256 devices in a mesh: ka: 8 (over z_hi, core), wa: 32 (over x, z_lo, y).
Axes of the slice: x: 4, y: 4, z: 8 (z_hi: 4, z_lo: 2; z = z_hi * 2 + z_lo), core: 2. Of those that a mesh axis runs over, the one named last changes fastest.
Arguments:
- coeff_val: bfloat16 [16, 128, 65536], P('ka', None, 'wa'), may hold values from -6 to 6
- coeff_cond: bfloat16 [16, 1024, 65536], P('ka', None, 'wa'), may hold values from -6 to 6
- miller: int32 [3, 65536], P(None, 'wa'), may hold values from -8 to 7
- energy_val: float32 [16, 128], P('ka'), may hold values from -12 to -1
- energy_cond: float32 [16, 1024], P('ka'), may hold values from 1 to 16
- orbit_val: bfloat16 [16, 128, 16384], P('ka', None, 'wa'), may hold values from -6 to 6
- orbit_cond: bfloat16 [16, 1024, 16384], P('ka', None, 'wa'), may hold values from -6 to 6
- zeta: bfloat16 [4096, 16384], P('wa'), may hold values from -0.046875 to 0.046875
- freqs: float32 [4], replicated, may hold values from 0.2 to 10
- kweight: int32 [16], P('ka'), may hold values from 1 to 8
Outputs:
- wing: float32 [3, 4, 4096], P(None, None, 'wa')
- head: float32 [3, 4], replicated
The draws below stay inside these ranges and needn't reach their ends.
All inputs are finite; a program needn't handle non-finite values.
Results may differ from the reference program's by a relative error of at most 0.008.
Values sent between devices are 32-bit elements; how exact they have to be, the bound alone decides.
No kernel may reach another device: no remote copies, remote signals or barrier semaphores. Data moves between devices by JAX's collectives and lax.ppermute only.
A program may use at most 128 MiB of HBM per device.

```python
import math
import jax
import jax.numpy as jnp
from jax import lax

V = 128
C = 1024
MU = 16384
G = 4096
NW = 4
NPW = 65536
NK = 16


def touch_ends(result, key, low, high):
    longest = result.shape.index(max(result.shape))
    spots = []
    for shift in (0, 1):
        where = [jax.random.randint(jax.random.fold_in(key, axis), (), 0, length) for axis, length in enumerate(result.shape)]
        where[longest] = (where[longest] + shift) % result.shape[longest]
        spots.append(tuple(where))
    return result.at[spots[0]].set(low).at[spots[1]].set(high)


def level_of(stream_key, dims, pieces, least, high):
    level, own = 1.0, jax.random.fold_in(stream_key, 6)
    for position, parts in pieces:
        heights = jnp.exp(jax.random.uniform(jax.random.fold_in(own, position), (parts,), jnp.float32, least / len(pieces), high / len(pieces)))
        level = level * jnp.repeat(heights, dims[position] // parts).reshape([-1 if axis == position else 1 for axis in range(len(dims))])
    return level


def centred(own_key, dims, scale, limit, cuts=(), held_as=jnp.bfloat16):
    drawn = jax.random.normal(own_key, dims, jnp.float32) * scale
    if len(cuts) > 0:
        drawn = level_of(own_key, dims, cuts, -0.22, 0.18) * drawn
    return jnp.clip(drawn, min=-limit, max=limit).astype(held_as)


def setup_inputs(seed: int = 0) -> dict:
    keys = jax.random.split(jax.random.key(seed), 11)
    return {
        "coeff_val": centred(keys[0], (NK, V, NPW), 1.0, 6.0, ((0, 8), (2, 32))),
        "coeff_cond": centred(keys[1], (NK, C, NPW), 1.0, 6.0, ((0, 8), (2, 32))),
        "miller": touch_ends(jax.random.randint(keys[2], (3, NPW), -8, 8), jax.random.fold_in(keys[2], 1), -8, 7).astype(jnp.int32),
        "energy_val": jnp.clip(-12.0 + 11.0 * jax.random.uniform(keys[3], (NK, V), jnp.float32) ** level_of(keys[3], (NK, V), ((0, 8),), -0.2, 0.2), -12.0, -1.0),
        "energy_cond": jnp.clip(1.0 + 15.0 * jax.random.uniform(keys[4], (NK, C), jnp.float32) ** level_of(keys[4], (NK, C), ((0, 8),), -0.2, 0.2), 1.0, 16.0),
        "orbit_val": centred(keys[5], (NK, V, MU), 1.0, 6.0, ((0, 8), (2, 32))),
        "orbit_cond": centred(keys[6], (NK, C, MU), 1.0, 6.0, ((0, 8), (2, 32))),
        "zeta": centred(keys[7], (G, MU), MU ** -0.5, 0.046875, ((0, 32),)),
        "freqs": jnp.clip(jnp.exp(jax.random.uniform(keys[8], (NW,), jnp.float32, math.log(0.2), math.log(10.0))), 0.2, 10.0),
        "kweight": touch_ends(jax.random.randint(keys[9], (NK,), 1, 9), jax.random.fold_in(keys[9], 1), 1, 8).astype(jnp.int32),
    }


def transition_factors(energy_gap, freqs):
    return 4.0 / (energy_gap[None] ** 2 + freqs[:, None, None] ** 2)


def reference(coeff_val, coeff_cond, miller, energy_val, energy_cond, orbit_val, orbit_cond, zeta, freqs, kweight):
    weights = kweight.astype(jnp.float32)
    weight_sum = jnp.sum(weights)
    momenta = miller.astype(jnp.float32)
    pw_factor = float(NPW) ** -0.5
    pair_factor = float(V * C) ** -0.5
    zeta_full = zeta.astype(jnp.float32)
    wing_acc = jnp.zeros((3 * NW, G), jnp.float32)
    head_acc = jnp.zeros((3, NW), jnp.float32)
    for kpoint in range(NK):
        weighted = (coeff_val[kpoint][None].astype(jnp.float32) * momenta[:, None, :]).astype(jnp.bfloat16)
        momentum = jnp.einsum("avg,cg->avc", weighted.astype(jnp.float32), coeff_cond[kpoint].astype(jnp.float32)) * pw_factor
        energy_gap = energy_cond[kpoint][None, :] - energy_val[kpoint][:, None]
        factors = transition_factors(energy_gap, freqs)
        head_term = jnp.sum(momentum[:, None] ** 2 * (factors / energy_gap[None])[None], axis=(2, 3)) / float(V * C)
        amplitude = (momentum[:, None] * factors[None]).astype(jnp.bfloat16).reshape(3 * NW, V, C)
        expanded = jnp.einsum("xvc,cm->xvm", amplitude.astype(jnp.float32), orbit_cond[kpoint].astype(jnp.float32))
        pair_sum = jnp.sum(orbit_val[kpoint].astype(jnp.float32)[None] * expanded, axis=1) * pair_factor
        wing_term = jnp.dot(pair_sum, zeta_full.T, precision=lax.Precision.HIGHEST, preferred_element_type=jnp.float32)
        wing_acc = wing_acc + weights[kpoint] * wing_term
        head_acc = head_acc + weights[kpoint] * head_term
    return (wing_acc / weight_sum).reshape(3, NW, G), head_acc / weight_sum
```

```python
import jax
import jax.numpy as jnp
from jax import lax
from jax.sharding import PartitionSpec as P


def split3(value):
    high = value.astype(jnp.bfloat16)
    rest = value - high.astype(jnp.float32)
    mid = rest.astype(jnp.bfloat16)
    low = (rest - mid.astype(jnp.float32)).astype(jnp.bfloat16)
    return high, mid, low


def everyone(value, axis):
    parts = lax.axis_size(axis)
    return lax.all_to_all(jnp.broadcast_to(value[None], (parts,) + value.shape), axis, 0, 0)


def local(
    coeff_val,
    coeff_cond,
    miller,
    energy_val,
    energy_cond,
    orbit_val,
    orbit_cond,
    zeta,
    freqs,
    kweight,
):
    kcount, nval, npw_dev = coeff_val.shape
    ncond = coeff_cond.shape[1]
    nfreq = freqs.shape[0]
    slab_rows = zeta.shape[0]
    ways = lax.axis_size("wa")
    rows = ncond // ways
    me = lax.axis_index("wa")
    points = orbit_val.shape[2]
    pw_factor = float(npw_dev * ways) ** (-0.5)
    pair_factor = float(nval * ncond) ** (-0.5)
    weights = kweight.astype(jnp.float32)
    momenta = miller.astype(jnp.float32)

    partials = []
    for kpoint in range(kcount):
        weighted = (coeff_val[kpoint][None] * momenta[:, None, :]).astype(jnp.bfloat16)
        partials.append(
            jnp.einsum("cg,avg->cav", coeff_cond[kpoint], weighted, preferred_element_type=jnp.float32)
        )
    partial_mom = jnp.stack(partials, axis=0).reshape(kcount, ways, rows, 3, nval)
    partial_mom = partial_mom.transpose(1, 0, 2, 3, 4)
    received = lax.all_to_all(partial_mom, "wa", 0, 0)
    mine = jnp.sum(received, axis=0) * pw_factor

    gap = energy_cond[:, :, None] - energy_val[:, None, :]
    factors = 4.0 / (gap[:, None] ** 2 + freqs[None, :, None, None] ** 2)

    my_gap = lax.dynamic_slice_in_dim(gap, me * rows, rows, 1)
    my_factors = lax.dynamic_slice_in_dim(factors, me * rows, rows, 2)
    ratio = weights[:, None, None, None] * my_factors / my_gap[:, None]
    head_part = jnp.einsum(
        "kcav,kwcv->aw", mine * mine, ratio, precision=lax.Precision.HIGHEST
    ) / float(nval * ncond)

    momentum = everyone(mine, "wa")
    momentum = momentum.transpose(1, 0, 2, 3, 4).reshape(kcount, ncond, 3, nval)
    pair = jnp.zeros((3 * nfreq, points), jnp.float32)
    for kpoint in range(kcount):
        amplitude = (
            momentum[kpoint][:, :, None, :] * factors[kpoint].transpose(1, 0, 2)[:, None]
        ).astype(jnp.bfloat16)
        expanded = jnp.einsum(
            "cxv,cm->xvm",
            amplitude.reshape(ncond, 3 * nfreq, nval),
            orbit_cond[kpoint],
            preferred_element_type=jnp.float32,
        )
        pair_k = jnp.sum(orbit_val[kpoint].astype(jnp.float32)[None] * expanded, axis=1)
        pair = pair + (weights[kpoint] * pair_factor) * pair_k

    tail = jnp.concatenate([head_part.reshape(-1), jnp.sum(weights)[None]])
    message = jnp.concatenate([pair, jnp.pad(tail, (0, points - tail.shape[0]))[None]], axis=0)
    gathered = everyone(message, "wa")
    tail = jnp.sum(gathered[:, 3 * nfreq, :slab_rows], axis=0)
    whole = gathered[:, : 3 * nfreq].transpose(1, 0, 2).reshape(3 * nfreq, ways * points)
    terms = lax.dot_general(
        jnp.concatenate(split3(whole), axis=0),
        zeta,
        (((1,), (1,)), ((), ())),
        preferred_element_type=jnp.float32,
    )
    wing = jnp.sum(terms.reshape(3, 3 * nfreq, slab_rows), axis=0)
    total = jnp.sum(everyone(jnp.concatenate([wing, tail[None]], axis=0), "ka"), axis=0)
    scale = 1.0 / (total[3 * nfreq, 3 * nfreq] / ways)
    wing = total[: 3 * nfreq] * scale
    head = total[3 * nfreq, : 3 * nfreq] * scale
    return wing.reshape(3, nfreq, slab_rows), head.reshape(3, nfreq)


def solution(mesh):
    return jax.shard_map(
        local,
        mesh=mesh,
        in_specs=(
            P("ka", None, "wa"),
            P("ka", None, "wa"),
            P(None, "wa"),
            P("ka", None),
            P("ka", None),
            P("ka", None, "wa"),
            P("ka", None, "wa"),
            P("wa", None),
            P(),
            P("ka"),
        ),
        out_specs=(P(None, None, "wa"), P()),
        check_vma=False,
    )
```

```python
import functools

import jax
import jax.numpy as jnp
from jax import lax
from jax.experimental import pallas as pl
from jax.experimental.pallas import tpu as pltpu
from jax.sharding import PartitionSpec as P

MASKS = ((8, 24, 1, 3, 4), (1, 3, 8, 24, 4))
CB, VB = 4, 8
F32, BF16 = jnp.float32, jnp.bfloat16
VMEM, SMEM = pl.BlockSpec(memory_space=pltpu.VMEM), pl.BlockSpec(memory_space=pltpu.SMEM)
QUARTERS = (((0, 0), (1, 0), (0, 1), (2, 1)), ((2, 0), (3, 0), (1, 1), (3, 1)))


def code_of(index, kpoint):
    x, z, y = index >> 3, (index >> 2) & 1, index & 3
    pairs_x = (((x ^ (x >> 1)) & 1) << 1) | (x >> 1)
    pairs_y = (((y ^ (y >> 1)) & 1) << 1) | (y >> 1)
    return (pairs_x, pairs_y << 1 | z) if kpoint == 0 else (pairs_y, pairs_x << 1 | z)


def swap(value, axis, mask):
    size = lax.axis_size(axis)
    return lax.ppermute(value, axis, [(i, i ^ mask) for i in range(size)])


def everyone(value, axis):
    parts = lax.axis_size(axis)
    return lax.all_to_all(jnp.broadcast_to(value[None], (parts,) + value.shape), axis, 0, 0)


def scattered(parts, masks):
    keep_a, send_a, keep_b, send_b = parts
    got_a, got_b = swap(send_a, "wa", masks[0]), swap(send_b, "wa", masks[1])
    send_a, send_b = keep_a[VB:] + got_a[VB:], keep_b[VB:] + got_b[VB:]
    keep_a, keep_b = keep_a[:VB] + got_a[:VB], keep_b[:VB] + got_b[:VB]
    got_a, got_b = swap(send_a, "wa", masks[1]), swap(send_b, "wa", masks[0])
    half = VB // 2
    keep = jnp.stack([keep_a[:half] + got_a[:half], keep_b[:half] + got_b[:half]])
    send = jnp.stack([keep_a[half:] + got_a[half:], keep_b[half:] + got_b[half:]])
    got = swap(send, "wa", masks[2])
    half = half // 2
    keep, send = keep[:, :half] + got[:, :half], keep[:, half:] + got[:, half:]
    return keep + swap(send, "wa", masks[3])


def gathered_chunks(held, masks):
    for mask in (masks[3], masks[2]):
        held = jnp.concatenate([held, swap(held, "wa", mask)], axis=1)
    held_a, held_b = held[0], held[1]
    got_a, got_b = swap(held_a, "wa", masks[1]), swap(held_b, "wa", masks[0])
    held_a, held_b = jnp.concatenate([held_a, got_a]), jnp.concatenate([held_b, got_b])
    got_a, got_b = swap(held_a, "wa", masks[0]), swap(held_b, "wa", masks[1])
    return (held_a, held_b), (got_a, got_b)


def momentum_kernel(kpoint, place_ref, val_ref, miller_ref, cond_ref, keep_a, send_a, keep_b, send_b, weighted):
    nval = val_ref.shape[0]
    rows = nval // VB
    cols = keep_a.shape[3]
    step = pl.program_id(0)
    _, me_v = code_of(place_ref[0], kpoint)

    @pl.when(step == 0)
    def _():
        for place in range(VB):
            source = pl.multiple_of((place ^ me_v) * rows, rows)
            block = val_ref[pl.ds(source, rows), :].astype(F32)
            for axis in range(3):
                factor = miller_ref[axis : axis + 1, :].astype(F32)
                weighted[axis * nval + place * rows : axis * nval + (place + 1) * rows, :] = (
                    block * factor
                ).astype(BF16)

    result = lax.dot_general(
        weighted[...], cond_ref[...], (((1,), (1,)), ((), ())), preferred_element_type=F32
    )

    def store(out, other, first):
        for eighth in range(VB):
            for axis in range(3):
                start = axis * nval + eighth * rows
                out[other * VB + eighth, axis] = result[start : start + rows, first : first + cols]

    high, low = step // 2, step % 2
    pl.when(high == 0)(lambda: store(keep_a, low, 0))
    pl.when(high == 1)(lambda: store(send_a, low, 0))
    pl.when(low == 0)(lambda: store(keep_b, high, cols))
    pl.when(low == 1)(lambda: store(send_b, high, cols))


def partial_momentum(kpoint, place, val, miller, cond):
    nval, depth = val.shape
    ncond = cond.shape[0]
    rows, cols = nval // VB, ncond // CB
    half = jax.ShapeDtypeStruct((CB * VB // 2, 3, rows, cols // 2), F32)
    return pl.pallas_call(
        functools.partial(momentum_kernel, kpoint),
        grid_spec=pltpu.PrefetchScalarGridSpec(
            num_scalar_prefetch=1,
            grid=(CB,),
            in_specs=[
                pl.BlockSpec((nval, depth), lambda i, me: (0, 0)),
                pl.BlockSpec((3, depth), lambda i, me: (0, 0)),
                pl.BlockSpec((cols, depth), lambda i, me: (i ^ code_of(me[0], kpoint)[0], 0)),
            ],
            out_specs=[pl.BlockSpec(half.shape, lambda i, me: (0, 0, 0, 0))] * 4,
            scratch_shapes=[pltpu.VMEM((3 * nval, depth), BF16)],
        ),
        out_shape=[half] * 4,
        cost_estimate=pl.CostEstimate(
            flops=2 * 3 * nval * ncond * depth,
            bytes_accessed=2 * (nval + ncond) * depth + 12 * nval * ncond,
            transcendentals=0,
        ),
        compiler_params=pltpu.CompilerParams(vmem_limit_bytes=20 << 20),
        name="partial_momentum",
    )(place, val, miller, cond)


def pair_kernel(half, place_ref, weight_ref, freq_ref, energy_val, energy_cond, orbit_val, orbit_cond, *refs):
    kcount, nval, points = orbit_val.shape
    ncond = orbit_cond.shape[1]
    nfreq = freq_ref.shape[0]
    chunks, refs = refs[: 2 * kcount], refs[2 * kcount :]
    before, refs = (refs[0], refs[1:]) if half else (None, refs)
    outs, (total, amplitude, level, orbits, weight) = refs[:-5], refs[-5:]
    rows, cols = chunks[0].shape[2:]
    scale = float(nval * ncond) ** (-0.5)
    tops = 3 * nfreq
    for k in range(kcount):
        me_c, me_v = code_of(place_ref[0], k)
        level[k] = jnp.transpose(jnp.broadcast_to(energy_val[k : k + 1, :], (nval, nval)))
        top = []
        for piece, (quarter, side) in enumerate(QUARTERS[half]):
            start = pl.multiple_of(((quarter ^ me_c) * 2 + side) * cols, cols)
            top.append(energy_cond[k : k + 1, pl.ds(start, cols)])
            orbits[k, piece * cols : (piece + 1) * cols, :] = orbit_cond[k, pl.ds(start, cols), :]

        def factors_of(gap):
            square = gap * gap
            return [4.0 / (square + freq_ref[w] * freq_ref[w]) for w in range(nfreq)]

        def eighth(place, carry, k=k, me_v=me_v, top=top):
            mine = pl.ds(pl.multiple_of(place * rows, rows), rows)
            theirs = pl.ds(pl.multiple_of((place ^ me_v) * rows, rows), rows)
            weight[k, mine, :] = orbit_val[k, theirs, :].astype(F32) * (weight_ref[k] * scale)
            bottom = level[k, theirs, :]
            for piece in range(4):
                factors = factors_of(top[piece] - bottom)
                for axis in range(3):
                    momentum = chunks[2 * k + piece // 2][(piece % 2) * VB + place, axis]
                    for w in range(nfreq):
                        start = pl.multiple_of((axis * nfreq + w) * nval + place * rows, rows)
                        amplitude[k, pl.ds(start, rows), piece * cols : (piece + 1) * cols] = (
                            momentum * factors[w]
                        ).astype(BF16)
            return carry

        lax.fori_loop(0, VB, eighth, 0, unroll=2)
        for axis in range(3):
            first = axis * nfreq * nval
            expanded = jnp.dot(
                amplitude[k, first : first + nfreq * nval, :], orbits[k], preferred_element_type=F32
            )
            for w in range(nfreq):
                row = slice(axis * nfreq + w, axis * nfreq + w + 1)
                value = jnp.sum(expanded[w * nval : (w + 1) * nval] * weight[k], axis=0, keepdims=True)
                if k > 0:
                    value = value + total[row, :]
                elif half:
                    value = value + before[row, :]
                total[row, :] = value

        if not half:
            bottom = level[k, pl.ds(pl.multiple_of(me_v * rows, rows), rows), :]
            for w in range(nfreq):
                lanes = slice(w * cols, (w + 1) * cols)
                for axis in range(3):
                    value = 0.0
                    for side in range(2):
                        gap = top[2 * side] - bottom
                        ratio = factors_of(gap)[w] / gap
                        momentum = chunks[2 * k + side][0, axis]
                        value = value + momentum * momentum * ratio
                    value = jnp.sum(value, axis=0, keepdims=True) * (weight_ref[k] / float(nval * ncond))
                    row = slice(tops + axis, tops + axis + 1)
                    total[row, lanes] = value + total[row, lanes] if k else value
            row = slice(tops + 3, tops + 4)
            value = jnp.full((1, points), weight_ref[k], F32)
            total[row, :] = value + total[row, :] if k else value
    if half:
        total[tops:, :] = before[tops:, :]
        keep, send = outs
        across = points // 2
        keep[...] = total[:, pl.ds(pl.multiple_of(place_ref[1] * across, across), across)]
        send[...] = total[:, pl.ds(pl.multiple_of((1 - place_ref[1]) * across, across), across)]
    else:
        outs[0][...] = total[...]


def pair_sums(half, place, weights, freqs, energy_val, energy_cond, orbit_val, orbit_cond, chunks, before):
    kcount, nval, points = orbit_val.shape
    ncond = orbit_cond.shape[1]
    nfreq = freqs.shape[0]
    height = 3 * nfreq + 4
    depth = ncond // 2
    operands = [energy_val, energy_cond, orbit_val, orbit_cond] + chunks + before
    if half:
        out_shape = [jax.ShapeDtypeStruct((height, points // 2), F32)] * 2
    else:
        out_shape = [jax.ShapeDtypeStruct((height, points), F32)]
    return pl.pallas_call(
        functools.partial(pair_kernel, half),
        out_shape=out_shape,
        in_specs=[SMEM] * 3 + [VMEM] * len(operands),
        out_specs=[VMEM] * len(out_shape),
        scratch_shapes=[
            pltpu.VMEM((height, points), F32),
            pltpu.VMEM((kcount, 3 * nfreq * nval, depth), BF16),
            pltpu.VMEM((kcount, nval, nval), F32),
            pltpu.VMEM((kcount, depth, points), BF16),
            pltpu.VMEM((kcount, nval, points), F32),
        ],
        cost_estimate=pl.CostEstimate(
            flops=kcount * 2 * 3 * nfreq * nval * depth * points,
            bytes_accessed=kcount * (12 * nval * depth + 4 * depth * points),
            transcendentals=0,
        ),
        compiler_params=pltpu.CompilerParams(vmem_limit_bytes=20 << 20),
        name="pair_sums",
    )(place, weights, freqs, *operands)


def wing_kernel(place_ref, gathered, zeta, out):
    ways, height, points = gathered.shape
    slab_rows = zeta.shape[0]
    tops = height - 4
    total = jnp.zeros((3 * height, slab_rows), F32)
    last = jnp.zeros((4, points), F32)
    for device in range(ways):
        value = gathered[device]
        last = last + value[tops:]
        pieces = []
        for _ in range(3):
            rounded = value.astype(BF16)
            pieces.append(rounded)
            value = value - rounded.astype(F32)
        start = pl.multiple_of((2 * device + place_ref[1]) * points, points)
        total = total + lax.dot_general(
            jnp.concatenate(pieces, axis=0),
            zeta[:, pl.ds(start, points)],
            (((1,), (1,)), ((), ())),
            preferred_element_type=F32,
        )
    total = total[:height] + total[height : 2 * height] + total[2 * height :]
    out[:tops] = total[:tops]
    lane = lax.broadcasted_iota(jnp.int32, (3, slab_rows), 1)
    across = points // 2
    head = jnp.zeros((3, slab_rows), F32)
    for tile in range(2):
        value = jnp.sum(last[:3, tile * across : (tile + 1) * across], axis=1, keepdims=True)
        head = jnp.where(lane == 2 * place_ref[1] + tile, value, head)
    out[tops : tops + 3] = head
    out[tops + 3 :] = last[3:, :slab_rows]


def wing_sums(place, gathered, zeta):
    ways, height, points = gathered.shape
    slab_rows = zeta.shape[0]
    return pl.pallas_call(
        wing_kernel,
        out_shape=jax.ShapeDtypeStruct((height, slab_rows), F32),
        in_specs=[SMEM, VMEM, VMEM],
        out_specs=VMEM,
        cost_estimate=pl.CostEstimate(
            flops=6 * height * slab_rows * ways * points,
            bytes_accessed=4 * slab_rows * ways * points + 4 * height * ways * points,
            transcendentals=0,
        ),
        compiler_params=pltpu.CompilerParams(vmem_limit_bytes=20 << 20),
        name="wing_sums",
    )(place, gathered, zeta)


def final_kernel(copies, one, two, wing, head):
    total = one[...] + two[...]
    tops = total.shape[0] - 4
    nfreq = wing.shape[1]
    scale = copies / total[tops + 3 :]
    for axis in range(3):
        wing[axis] = total[axis * nfreq : (axis + 1) * nfreq] * scale
    head[...] = total[tops : tops + 3, :nfreq] * scale[:, :nfreq]


def local(
    coeff_val,
    coeff_cond,
    miller,
    energy_val,
    energy_cond,
    orbit_val,
    orbit_cond,
    zeta,
    freqs,
    kweight,
):
    kcount, nval, npw_dev = coeff_val.shape
    nfreq = freqs.shape[0]
    slab_rows = zeta.shape[0]
    ways = lax.axis_size("wa")
    pw_factor = float(npw_dev * ways) ** (-0.5)
    weights = kweight.astype(F32)
    place = jnp.stack([lax.axis_index("wa"), lax.axis_index("ka") & 1]).astype(jnp.int32)

    mine = []
    for k in range(kcount):
        parts = partial_momentum(k, place, coeff_val[k], miller, coeff_cond[k])
        mine.append(scattered(parts, MASKS[k]))
    mine = jnp.stack(mine)
    mine = (mine + swap(mine, "wa", MASKS[0][4])[:, :, ::-1]) * pw_factor

    chunks = [gathered_chunks(mine[k], MASKS[k]) for k in range(kcount)]
    operands = (place, weights, freqs, energy_val, energy_cond, orbit_val, orbit_cond)
    (pair,) = pair_sums(0, *operands, [part for k in range(kcount) for part in chunks[k][0]], [])
    keep, send = pair_sums(1, *operands, [part for k in range(kcount) for part in chunks[k][1]], [pair])
    pair = keep + swap(send, "ka", 1)
    total = wing_sums(place, everyone(pair, "wa"), zeta)
    total = total + swap(total, "ka", 1)
    total = total + swap(total, "ka", 2)
    return pl.pallas_call(
        functools.partial(final_kernel, float(2 * ways)),
        out_shape=[
            jax.ShapeDtypeStruct((3, nfreq, slab_rows), F32),
            jax.ShapeDtypeStruct((3, nfreq), F32),
        ],
        in_specs=[VMEM] * 2,
        out_specs=[VMEM] * 2,
        name="final",
    )(total, swap(total, "ka", 6))


def solution(mesh):
    return jax.shard_map(
        local,
        mesh=mesh,
        in_specs=(
            P("ka", None, "wa"),
            P("ka", None, "wa"),
            P(None, "wa"),
            P("ka", None),
            P("ka", None),
            P("ka", None, "wa"),
            P("ka", None, "wa"),
            P("wa", None),
            P(),
            P("ka"),
        ),
        out_specs=(P(None, None, "wa"), P()),
        check_vma=False,
    )
```

```python
import functools

import jax
import jax.numpy as jnp
from jax import lax
from jax.experimental import pallas as pl
from jax.experimental.pallas import tpu as pltpu
from jax.sharding import PartitionSpec as P

MASKS = (((8, 24, 1, 3, 4), (1, 3, 8, 24, 4)), ((24, 8, 1, 3, 4), (3, 1, 8, 24, 4)))
CB, VB = 4, 8
F32, BF16 = jnp.float32, jnp.bfloat16
VMEM, SMEM = pl.BlockSpec(memory_space=pltpu.VMEM), pl.BlockSpec(memory_space=pltpu.SMEM)
HBM = pl.BlockSpec(memory_space=pltpu.HBM)


def code_of(place, kpoint):
    index, core = place[0], place[1]
    x, z, y = index >> 3, (index >> 2) & 1, index & 3

    first, second = x + (y - x) * core, y + (x - y) * core
    one, two = (first ^ (first >> 1)) & 1, first >> 1
    quarter = one << 1 | two if kpoint == 0 else two << 1 | one
    return quarter, ((second ^ (second >> 1)) & 1) << 2 | (second >> 1) << 1 | z


def swap(value, axis, mask):
    return lax.ppermute(value, axis, [(i, i ^ mask) for i in range(lax.axis_size(axis))])


def cross(value, kpoint, dim):
    groups, ways = lax.axis_size("ka"), lax.axis_size("wa")
    pairs = [
        (group * ways + i, group * ways + (i ^ MASKS[kpoint][group & 1][dim]))
        for group in range(groups)
        for i in range(ways)
    ]
    return lax.ppermute(value, ("ka", "wa"), pairs)


def everyone(value, axis):
    parts = lax.axis_size(axis)
    return lax.all_to_all(jnp.broadcast_to(value[None], (parts,) + value.shape), axis, 0, 0)


def scattered(parts):
    held = []
    for kpoint, (keep, send) in enumerate(parts):
        got = cross(send, kpoint, 0)
        half = keep.shape[0] // 2
        more = cross(keep[half:] + got[half:], kpoint, 1)
        held.append((keep[:half] + got[:half], more))
    half = held[0][0].shape[0] // 2
    keep = jnp.stack([own[:half] + got[:half] for own, got in held])
    send = jnp.stack([own[half:] + got[half:] for own, got in held])
    got = cross(send, 0, 2)
    half = half // 2
    keep, send = keep[:, :half] + got[:, :half], keep[:, half:] + got[:, half:]
    return keep + cross(send, 0, 3)


def gathered_chunks(held):
    for dim in (3, 2):
        held = jnp.concatenate([held, cross(held, 0, dim)], axis=1)
    halves = []
    for kpoint in range(held.shape[0]):
        own = jnp.concatenate([held[kpoint], cross(held[kpoint], kpoint, 1)])
        halves.append((own, cross(own, kpoint, 0)))
    return halves


def momentum_kernel(kpoint, half, place_ref, miller_ref, val_ref, cond_ref, out, weighted, values, blocks, value_sems, sems):
    nval = values.shape[0]
    rows = nval // VB
    cols = out.shape[3]
    me_c, me_v = code_of(place_ref, kpoint)
    piece = nval // value_sems.shape[0]
    value_copies, copies = [], []
    for number in range(value_sems.shape[0]):
        lines = pl.ds(number * piece, piece)
        value_copies.append(
            pltpu.make_async_copy(val_ref.at[kpoint, lines], values.at[lines], value_sems.at[number])
        )
    for part in range(2):
        start = ((2 * half + part) ^ me_c) * cols
        piece = cols // sems.shape[1]
        for number in range(sems.shape[1]):
            source = pl.ds(pl.multiple_of(start + number * piece, piece), piece)
            copies.append(
                pltpu.make_async_copy(
                    cond_ref.at[kpoint, source],
                    blocks.at[part, pl.ds(number * piece, piece)],
                    sems.at[part, number],
                )
            )
    for copy in value_copies + copies:
        copy.start()
    for copy in value_copies:
        copy.wait()
    for place in range(VB):
        source = pl.multiple_of((place ^ me_v) * rows, rows)
        block = values[pl.ds(source, rows), :].astype(F32)
        for axis in range(3):
            factor = miller_ref[axis : axis + 1, :].astype(F32)
            weighted[axis * nval + place * rows : axis * nval + (place + 1) * rows, :] = (
                block * factor
            ).astype(BF16)
    for part in range(2):
        for copy in copies[part * sems.shape[1] : (part + 1) * sems.shape[1]]:
            copy.wait()
        result = lax.dot_general(
            weighted[...], blocks[part], (((1,), (1,)), ((), ())), preferred_element_type=F32
        )
        for eighth in range(VB):
            for axis in range(3):
                start = axis * nval + eighth * rows
                out[part * VB + eighth, axis] = result[start : start + rows]


def partial_momentum(kpoint, half, place, coeff_val, miller, coeff_cond):
    _, nval, depth = coeff_val.shape
    ncond = coeff_cond.shape[1]
    rows, cols = nval // VB, ncond // CB
    return pl.pallas_call(
        functools.partial(momentum_kernel, kpoint, half),
        out_shape=jax.ShapeDtypeStruct((CB * VB // 2, 3, rows, cols), F32),
        in_specs=[SMEM, VMEM, HBM, HBM],
        out_specs=VMEM,
        scratch_shapes=[
            pltpu.VMEM((3 * nval, depth), BF16),
            pltpu.VMEM((nval, depth), BF16),
            pltpu.VMEM((2, cols, depth), BF16),
            pltpu.SemaphoreType.DMA((4,)),
            pltpu.SemaphoreType.DMA((2, 8)),
        ],
        cost_estimate=pl.CostEstimate(
            flops=3 * nval * ncond * depth,
            bytes_accessed=(2 * nval + ncond) * depth + 6 * nval * ncond,
            transcendentals=0,
        ),
        compiler_params=pltpu.CompilerParams(vmem_limit_bytes=56 << 20),
        name="momentum_to_send" if half else "momentum_to_keep",
    )(place, miller, coeff_val, coeff_cond)


def pair_kernel(half, kpoints, place_ref, weight_ref, freq_ref, energy_val, energy_cond, orbit_val, orbit_cond, *refs):
    _, nval, points = orbit_val.shape
    ncond = orbit_cond.shape[1]
    nfreq = freq_ref.shape[0]
    count = len(kpoints)
    chunks, refs = refs[:count], refs[count:]
    before, refs = (refs[0], refs[1:]) if half else (None, refs)
    outs, (total, amplitude, level, orbits, weight) = refs[:-5], refs[-5:]
    rows, cols = chunks[0].shape[2:]
    scale = float(nval * ncond) ** (-0.5)
    tops = 3 * nfreq
    for spot, k in enumerate(kpoints):
        chunk = chunks[spot]
        me_c, me_v = code_of(place_ref, k)
        level[spot] = jnp.transpose(jnp.broadcast_to(energy_val[k : k + 1, :], (nval, nval)))
        top = []
        for part in range(2):
            start = pl.multiple_of(((2 * half + part) ^ me_c) * cols, cols)
            top.append(energy_cond[k : k + 1, pl.ds(start, cols)])
            orbits[spot, part * cols : (part + 1) * cols, :] = orbit_cond[k, pl.ds(start, cols), :]

        def bottom_of(where, spot=spot):
            return jnp.concatenate([level[spot, where, :]] * (cols // nval), axis=1)

        def factors_of(gap):
            square = gap * gap
            return [4.0 / (square + freq_ref[w] * freq_ref[w]) for w in range(nfreq)]

        def eighth(place, carry, k=k, spot=spot, me_v=me_v, top=top, chunk=chunk, bottom_of=bottom_of):
            mine = pl.ds(pl.multiple_of(place * rows, rows), rows)
            theirs = pl.ds(pl.multiple_of((place ^ me_v) * rows, rows), rows)
            weight[spot, mine, :] = orbit_val[k, theirs, :].astype(F32) * (weight_ref[k] * scale)
            bottom = bottom_of(theirs)
            for part in range(2):
                factors = factors_of(top[part] - bottom)
                for axis in range(3):
                    momentum = chunk[part * VB + place, axis]
                    for w in range(nfreq):
                        start = pl.multiple_of((axis * nfreq + w) * nval + place * rows, rows)
                        amplitude[spot, pl.ds(start, rows), part * cols : (part + 1) * cols] = (
                            momentum * factors[w]
                        ).astype(BF16)
            return carry

        lax.fori_loop(0, VB, eighth, 0, unroll=2)
        for axis in range(3):
            first = axis * nfreq * nval
            expanded = jnp.dot(
                amplitude[spot, first : first + nfreq * nval, :], orbits[spot], preferred_element_type=F32
            )
            for w in range(nfreq):
                row = slice(axis * nfreq + w, axis * nfreq + w + 1)
                value = jnp.sum(expanded[w * nval : (w + 1) * nval] * weight[spot], axis=0, keepdims=True)
                if spot > 0:
                    value = value + total[row, :]
                elif half:
                    value = value + before[row, :]
                total[row, :] = value

        if not half:
            bottom = bottom_of(pl.ds(pl.multiple_of(me_v * rows, rows), rows))
            gap = top[0] - bottom
            ratios = [factor / gap for factor in factors_of(gap)]
            for axis in range(3):
                square = chunk[0, axis] * chunk[0, axis]
                row = slice(tops + axis, tops + axis + 1)
                for w in range(nfreq):
                    value = jnp.sum(square * ratios[w], axis=0, keepdims=True)
                    value = (value[:, :nval] + value[:, nval:]) * (weight_ref[k] / float(nval * ncond))
                    lanes = slice(w * nval, (w + 1) * nval)
                    total[row, lanes] = value + total[row, lanes] if spot else value
            row = slice(tops + 3, tops + 4)
            value = jnp.full((1, points), weight_ref[k], F32)
            total[row, :] = value + total[row, :] if spot else value
    if half:
        total[tops:, :] = before[tops:, :]
    if len(outs) == 2:
        keep, send = outs
        across = points // 2
        keep[...] = total[:, pl.ds(pl.multiple_of(place_ref[1] * across, across), across)]
        send[...] = total[:, pl.ds(pl.multiple_of((1 - place_ref[1]) * across, across), across)]
    else:
        outs[0][...] = total[...]


def pair_sums(half, kpoints, place, weights, freqs, energy_val, energy_cond, orbit_val, orbit_cond, chunks, before, parts):
    _, nval, points = orbit_val.shape
    ncond = orbit_cond.shape[1]
    nfreq = freqs.shape[0]
    height = 3 * nfreq + 4
    depth = ncond // 2
    count = len(kpoints)
    operands = [energy_val, energy_cond, orbit_val, orbit_cond, *chunks, *before]
    return pl.pallas_call(
        functools.partial(pair_kernel, half, kpoints),
        out_shape=[jax.ShapeDtypeStruct((height, points // parts), F32)] * parts,
        in_specs=[SMEM] * 3 + [VMEM] * len(operands),
        out_specs=[VMEM] * parts,
        scratch_shapes=[
            pltpu.VMEM((height, points), F32),
            pltpu.VMEM((count, 3 * nfreq * nval, depth), BF16),
            pltpu.VMEM((count, nval, nval), F32),
            pltpu.VMEM((count, depth, points), BF16),
            pltpu.VMEM((count, nval, points), F32),
        ],
        cost_estimate=pl.CostEstimate(
            flops=count * 2 * 3 * nfreq * nval * depth * points,
            bytes_accessed=count * (12 * nval * depth + 4 * depth * points),
            transcendentals=0,
        ),
        compiler_params=pltpu.CompilerParams(vmem_limit_bytes=20 << 20),
        name="pair_sums",
    )(place, weights, freqs, *operands)


def wing_kernel(place_ref, gathered, zeta, out):
    ways, height, points = gathered.shape
    slab_rows = zeta.shape[0]
    tops = height - 4
    total = jnp.zeros((3 * height, slab_rows), F32)
    last = jnp.zeros((4, points), F32)
    for device in range(ways):
        value = gathered[device]
        last = last + value[tops:]
        pieces = []
        for _ in range(3):
            rounded = value.astype(BF16)
            pieces.append(rounded)
            value = value - rounded.astype(F32)
        start = pl.multiple_of((2 * device + place_ref[1]) * points, points)
        total = total + lax.dot_general(
            jnp.concatenate(pieces, axis=0),
            zeta[:, pl.ds(start, points)],
            (((1,), (1,)), ((), ())),
            preferred_element_type=F32,
        )
    total = total[:height] + total[height : 2 * height] + total[2 * height :]
    out[:tops] = total[:tops]
    lane = lax.broadcasted_iota(jnp.int32, (3, slab_rows), 1)
    across = points // 2
    head = jnp.zeros((3, slab_rows), F32)
    for tile in range(2):
        value = jnp.sum(last[:3, tile * across : (tile + 1) * across], axis=1, keepdims=True)
        head = jnp.where(lane == 2 * place_ref[1] + tile, value, head)
    out[tops : tops + 3] = head
    out[tops + 3 :] = last[3:, :slab_rows]


def wing_sums(place, gathered, zeta):
    ways, height, points = gathered.shape
    slab_rows = zeta.shape[0]
    return pl.pallas_call(
        wing_kernel,
        out_shape=jax.ShapeDtypeStruct((height, slab_rows), F32),
        in_specs=[SMEM, VMEM, VMEM],
        out_specs=VMEM,
        cost_estimate=pl.CostEstimate(
            flops=6 * height * slab_rows * ways * points,
            bytes_accessed=4 * slab_rows * ways * points + 4 * height * ways * points,
            transcendentals=0,
        ),
        compiler_params=pltpu.CompilerParams(vmem_limit_bytes=20 << 20),
        name="wing_sums",
    )(place, gathered, zeta)


def final_kernel(copies, one, two, three, four, wing, head):
    total = (one[...] + two[...]) + (three[...] + four[...])
    tops = total.shape[0] - 4
    nfreq = wing.shape[1]
    scale = copies / total[tops + 3 :]
    for axis in range(3):
        wing[axis] = total[axis * nfreq : (axis + 1) * nfreq] * scale
    head[...] = total[tops : tops + 3, :nfreq] * scale[:, :nfreq]


def local(
    coeff_val,
    coeff_cond,
    miller,
    energy_val,
    energy_cond,
    orbit_val,
    orbit_cond,
    zeta,
    freqs,
    kweight,
):
    kcount, nval, npw_dev = coeff_val.shape
    nfreq = freqs.shape[0]
    slab_rows = zeta.shape[0]
    ways = lax.axis_size("wa")
    pw_factor = float(npw_dev * ways) ** (-0.5)
    weights = kweight.astype(F32)
    place = jnp.stack([lax.axis_index("wa"), lax.axis_index("ka") & 1]).astype(jnp.int32)

    sends = [partial_momentum(k, 1, place, coeff_val, miller, coeff_cond) for k in range(kcount)]
    keeps = [partial_momentum(k, 0, place, coeff_val, miller, coeff_cond) for k in range(kcount)]
    mine = scattered(list(zip(keeps, sends)))
    mine = (mine + swap(mine, "wa", MASKS[0][0][4])[:, ::-1]) * pw_factor

    (own_0, got_0), (own_1, got_1) = gathered_chunks(mine)
    operands = (place, weights, freqs, energy_val, energy_cond, orbit_val, orbit_cond)
    pair = pair_sums(0, (0, 1), *operands, [own_0, own_1], [], 1)
    pair = pair_sums(1, (0,), *operands, [got_0], pair, 1)
    keep, send = pair_sums(1, (1,), *operands, [got_1], pair, 2)
    pair = keep + swap(send, "ka", 1)
    total = wing_sums(place, everyone(pair, "wa"), zeta)
    total = total + swap(total, "ka", 1)
    return pl.pallas_call(
        functools.partial(final_kernel, float(2 * ways)),
        out_shape=[
            jax.ShapeDtypeStruct((3, nfreq, slab_rows), F32),
            jax.ShapeDtypeStruct((3, nfreq), F32),
        ],
        in_specs=[VMEM] * 4,
        out_specs=[VMEM] * 2,
        compiler_params=pltpu.CompilerParams(vmem_limit_bytes=4 << 20),
        name="final",
    )(total, *[swap(total, "ka", mask) for mask in (2, 4, 6)])


def solution(mesh):
    return jax.shard_map(
        local,
        mesh=mesh,
        in_specs=(
            P("ka", None, "wa"),
            P("ka", None, "wa"),
            P(None, "wa"),
            P("ka", None),
            P("ka", None),
            P("ka", None, "wa"),
            P("ka", None, "wa"),
            P("wa", None),
            P(),
            P("ka"),
        ),
        out_specs=(P(None, None, "wa"), P()),
        check_vma=False,
    )
```

```python
import functools

import jax
import jax.numpy as jnp
from jax import lax
from jax.experimental import pallas as pl
from jax.experimental.pallas import tpu as pltpu
from jax.sharding import PartitionSpec as P

MASKS = (((8, 24, 1, 3, 4), (1, 3, 8, 24, 4)), ((24, 8, 1, 3, 4), (3, 1, 8, 24, 4)))
CB, VB = 4, 8
F32, BF16 = jnp.float32, jnp.bfloat16
VMEM, SMEM = pl.BlockSpec(memory_space=pltpu.VMEM), pl.BlockSpec(memory_space=pltpu.SMEM)

def code_of(place, kpoint):
    index, core = place[0], place[1]
    x, z, y = index >> 3, (index >> 2) & 1, index & 3

    first, second = x + (y - x) * core, y + (x - y) * core
    one, two = (first ^ (first >> 1)) & 1, first >> 1
    quarter = one << 1 | two if kpoint == 0 else two << 1 | one
    return quarter, ((second ^ (second >> 1)) & 1) << 2 | (second >> 1) << 1 | z


def swap(value, axis, mask):
    return lax.ppermute(value, axis, [(i, i ^ mask) for i in range(lax.axis_size(axis))])


def cross(value, kpoint, *dims):
    groups, ways = lax.axis_size("ka"), lax.axis_size("wa")
    pairs = []
    for group in range(groups):
        mask = 0
        for dim in dims:
            mask ^= MASKS[kpoint][group & 1][dim]
        pairs += [(group * ways + i, group * ways + (i ^ mask)) for i in range(ways)]
    return lax.ppermute(value, ("ka", "wa"), pairs)


def everyone(value, axis):
    parts = lax.axis_size(axis)
    return lax.all_to_all(jnp.broadcast_to(value[None], (parts,) + value.shape), axis, 0, 0)


def scattered(parts):
    held = []
    for kpoint, (own, second, first, both) in enumerate(parts):
        second = second + cross(both, kpoint, 0)
        held.append((own, cross(first, kpoint, 0), cross(second, kpoint, 1)))

    def summed(place):
        lines = slice(2 * place, 2 * place + 2)
        return jnp.stack([(own[lines] + one[lines]) + two[lines] for own, one, two in held])

    return (summed(0) + cross(summed(2), 0, 2)) + (cross(summed(1), 0, 3) + cross(summed(3), 0, 2, 3))


def gathered_chunks(held):
    others = [cross(held, 0, *dims) for dims in ((3,), (2,), (2, 3))]
    held = jnp.concatenate([held] + others, axis=1)
    quarters = []
    for kpoint in range(held.shape[0]):
        own = held[kpoint]
        first, second = cross(own, kpoint, 0), cross(own, kpoint, 1)
        quarters.append((own, second, first, cross(first, kpoint, 1)))
    return quarters


def momentum_kernel(kpoint, quarters, place_ref, val_ref, miller_ref, cond_ref, *refs):
    outs, weighted = refs[:-1], refs[-1]
    nval = val_ref.shape[1]
    rows, cols = outs[0].shape[2:]
    me_c, me_v = code_of(place_ref, kpoint)
    for place in range(VB):
        source = pl.multiple_of((place ^ me_v) * rows, rows)
        block = val_ref[kpoint, pl.ds(source, rows), :].astype(F32)
        for axis in range(3):
            factor = miller_ref[axis : axis + 1, :].astype(F32)
            weighted[axis * nval + place * rows : axis * nval + (place + 1) * rows, :] = (
                block * factor
            ).astype(BF16)
    for quarter, out in zip(quarters, outs):
        start = pl.multiple_of((quarter ^ me_c) * cols, cols)
        result = lax.dot_general(
            weighted[...],
            cond_ref[kpoint, pl.ds(start, cols), :],
            (((1,), (1,)), ((), ())),
            preferred_element_type=F32,
        )
        for eighth in range(VB):
            for axis in range(3):
                start = axis * nval + eighth * rows
                out[eighth, axis] = result[start : start + rows]


def partial_momentum(kpoint, quarters, place, coeff_val, miller, coeff_cond):
    _, nval, depth = coeff_val.shape
    ncond = coeff_cond.shape[1]
    count = len(quarters)
    return pl.pallas_call(
        functools.partial(momentum_kernel, kpoint, quarters),
        out_shape=[jax.ShapeDtypeStruct((VB, 3, nval // VB, ncond // CB), F32)] * count,
        in_specs=[SMEM, VMEM, VMEM, VMEM],
        out_specs=[VMEM] * count,
        scratch_shapes=[pltpu.VMEM((3 * nval, depth), BF16)],
        cost_estimate=pl.CostEstimate(
            flops=2 * 3 * nval * ncond * depth * count // CB,
            bytes_accessed=(2 * nval + 2 * ncond * count // CB) * depth + 12 * nval * ncond * count // CB,
            transcendentals=0,
        ),
        compiler_params=pltpu.CompilerParams(vmem_limit_bytes=24 << 20),
        name="partial_momentum",
    )(place, coeff_val, miller, coeff_cond)


def pair_kernel(groups, place_ref, weight_ref, freq_ref, energy_val, energy_cond, orbit_val, orbit_cond, *refs):
    _, nval, points = orbit_val.shape
    ncond = orbit_cond.shape[1]
    nfreq = freq_ref.shape[0]
    count = sum(len(quarters) for _, quarters in groups)
    chunks, refs = refs[:count], refs[count:]
    begins = groups[0][1][0] == 0
    before, refs = (None, refs) if begins else (refs[0], refs[1:])
    outs, (total, amplitude, level, orbits, weight) = refs[:-5], refs[-5:]
    rows, cols = chunks[0].shape[2:]
    scale = float(nval * ncond) ** (-0.5)
    tops = 3 * nfreq
    for spot, (k, quarters) in enumerate(groups):
        mine, chunks = chunks[: len(quarters)], chunks[len(quarters) :]
        depth = len(quarters) * cols
        me_c, me_v = code_of(place_ref, k)
        level[spot] = jnp.transpose(jnp.broadcast_to(energy_val[k : k + 1, :], (nval, nval)))
        top = []
        for part, quarter in enumerate(quarters):
            start = pl.multiple_of((quarter ^ me_c) * cols, cols)
            top.append(energy_cond[k : k + 1, pl.ds(start, cols)])
            orbits[spot, part * cols : (part + 1) * cols, :] = orbit_cond[k, pl.ds(start, cols), :]

        def bottom_of(where, spot=spot):
            return jnp.concatenate([level[spot, where, :]] * (cols // nval), axis=1)

        def factors_of(gap):
            square = gap * gap
            return [4.0 / (square + freq_ref[w] * freq_ref[w]) for w in range(nfreq)]

        def eighth(place, carry, k=k, spot=spot, me_v=me_v, top=top, mine=mine, bottom_of=bottom_of):
            here = pl.ds(pl.multiple_of(place * rows, rows), rows)
            there = pl.ds(pl.multiple_of((place ^ me_v) * rows, rows), rows)
            weight[spot, here, :] = orbit_val[k, there, :].astype(F32) * (weight_ref[k] * scale)
            bottom = bottom_of(there)
            for part, chunk in enumerate(mine):
                factors = factors_of(top[part] - bottom)
                for axis in range(3):
                    momentum = chunk[place, axis]
                    for w in range(nfreq):
                        start = pl.multiple_of((axis * nfreq + w) * nval + place * rows, rows)
                        amplitude[spot, pl.ds(start, rows), part * cols : (part + 1) * cols] = (
                            momentum * factors[w]
                        ).astype(BF16)
            return carry

        lax.fori_loop(0, VB, eighth, 0, unroll=2)
        for axis in range(3):
            start = axis * nfreq * nval
            expanded = jnp.dot(
                amplitude[spot, start : start + nfreq * nval, :depth],
                orbits[spot, :depth, :],
                preferred_element_type=F32,
            )
            for w in range(nfreq):
                row = slice(axis * nfreq + w, axis * nfreq + w + 1)
                value = jnp.sum(expanded[w * nval : (w + 1) * nval] * weight[spot], axis=0, keepdims=True)
                if spot > 0:
                    value = value + total[row, :]
                elif not begins:
                    value = value + before[row, :]
                total[row, :] = value

        if begins:
            bottom = bottom_of(pl.ds(pl.multiple_of(me_v * rows, rows), rows))
            gap = top[0] - bottom
            ratios = [factor / gap for factor in factors_of(gap)]
            for axis in range(3):
                square = mine[0][0, axis] * mine[0][0, axis]
                row = slice(tops + axis, tops + axis + 1)
                for w in range(nfreq):
                    value = jnp.sum(square * ratios[w], axis=0, keepdims=True)
                    value = (value[:, :nval] + value[:, nval:]) * (weight_ref[k] / float(nval * ncond))
                    lanes = slice(w * nval, (w + 1) * nval)
                    total[row, lanes] = value + total[row, lanes] if spot else value
            row = slice(tops + 3, tops + 4)
            value = jnp.full((1, points), weight_ref[k], F32)
            total[row, :] = value + total[row, :] if spot else value
    if not begins:
        total[tops:, :] = before[tops:, :]
    if len(outs) == 2:
        keep, send = outs
        across = points // 2
        keep[...] = total[:, pl.ds(pl.multiple_of(place_ref[1] * across, across), across)]
        send[...] = total[:, pl.ds(pl.multiple_of((1 - place_ref[1]) * across, across), across)]
    else:
        outs[0][...] = total[...]


def pair_sums(groups, place, weights, freqs, energy_val, energy_cond, orbit_val, orbit_cond, chunks, before, parts):
    _, nval, points = orbit_val.shape
    ncond = orbit_cond.shape[1]
    nfreq = freqs.shape[0]
    height = 3 * nfreq + 4
    depth = ncond // CB * max(len(quarters) for _, quarters in groups)
    count = len(groups)
    operands = [energy_val, energy_cond, orbit_val, orbit_cond]
    operands += [chunks[k][quarter] for k, quarters in groups for quarter in quarters]
    operands += before
    return list(
        pl.pallas_call(
            functools.partial(pair_kernel, groups),
            out_shape=[jax.ShapeDtypeStruct((height, points // parts), F32)] * parts,
            in_specs=[SMEM] * 3 + [VMEM] * len(operands),
            out_specs=[VMEM] * parts,
            scratch_shapes=[
                pltpu.VMEM((height, points), F32),
                pltpu.VMEM((count, 3 * nfreq * nval, depth), BF16),
                pltpu.VMEM((count, nval, nval), F32),
                pltpu.VMEM((count, depth, points), BF16),
                pltpu.VMEM((count, nval, points), F32),
            ],
            cost_estimate=pl.CostEstimate(
                flops=count * 2 * 3 * nfreq * nval * depth * points,
                bytes_accessed=count * (12 * nval * depth + 4 * depth * points),
                transcendentals=0,
            ),
            compiler_params=pltpu.CompilerParams(vmem_limit_bytes=20 << 20),
            name="pair_sums",
        )(place, weights, freqs, *operands)
    )


def wing_kernel(place_ref, gathered, zeta, out):
    ways, height, points = gathered.shape
    slab_rows = zeta.shape[0]
    tops = height - 4
    total = jnp.zeros((3 * height, slab_rows), F32)
    last = jnp.zeros((4, points), F32)
    for device in range(ways):
        value = gathered[device]
        last = last + value[tops:]
        pieces = []
        for _ in range(3):
            rounded = value.astype(BF16)
            pieces.append(rounded)
            value = value - rounded.astype(F32)
        start = pl.multiple_of((2 * device + place_ref[1]) * points, points)
        total = total + lax.dot_general(
            jnp.concatenate(pieces, axis=0),
            zeta[:, pl.ds(start, points)],
            (((1,), (1,)), ((), ())),
            preferred_element_type=F32,
        )
    total = total[:height] + total[height : 2 * height] + total[2 * height :]
    out[:tops] = total[:tops]
    lane = lax.broadcasted_iota(jnp.int32, (3, slab_rows), 1)
    across = points // 2
    head = jnp.zeros((3, slab_rows), F32)
    for tile in range(2):
        value = jnp.sum(last[:3, tile * across : (tile + 1) * across], axis=1, keepdims=True)
        head = jnp.where(lane == 2 * place_ref[1] + tile, value, head)
    out[tops : tops + 3] = head
    out[tops + 3 :] = last[3:, :slab_rows]


def wing_sums(place, gathered, zeta):
    ways, height, points = gathered.shape
    slab_rows = zeta.shape[0]
    return pl.pallas_call(
        wing_kernel,
        out_shape=jax.ShapeDtypeStruct((height, slab_rows), F32),
        in_specs=[SMEM, VMEM, VMEM],
        out_specs=VMEM,
        cost_estimate=pl.CostEstimate(
            flops=6 * height * slab_rows * ways * points,
            bytes_accessed=4 * slab_rows * ways * points + 4 * height * ways * points,
            transcendentals=0,
        ),
        compiler_params=pltpu.CompilerParams(vmem_limit_bytes=20 << 20),
        name="wing_sums",
    )(place, gathered, zeta)


def final_kernel(copies, one, two, wing, head):
    total = one[...] + two[...]
    tops = total.shape[0] - 4
    nfreq = wing.shape[1]
    scale = copies / total[tops + 3 :]
    for axis in range(3):
        wing[axis] = total[axis * nfreq : (axis + 1) * nfreq] * scale
    head[...] = total[tops : tops + 3, :nfreq] * scale[:, :nfreq]


def local(
    coeff_val,
    coeff_cond,
    miller,
    energy_val,
    energy_cond,
    orbit_val,
    orbit_cond,
    zeta,
    freqs,
    kweight,
):
    kcount, nval, npw_dev = coeff_val.shape
    nfreq = freqs.shape[0]
    slab_rows = zeta.shape[0]
    ways = lax.axis_size("wa")
    pw_factor = float(npw_dev * ways) ** (-0.5)
    weights = kweight.astype(F32)
    place = jnp.stack([lax.axis_index("wa"), lax.axis_index("ka") & 1]).astype(jnp.int32)

    operands = (place, coeff_val, miller, coeff_cond)
    sends = [partial_momentum(k, (3, 2), *operands) for k in range(kcount)]
    keeps = [partial_momentum(k, (1, 0), *operands) for k in range(kcount)]
    parts = [(own, second, first, both) for (both, first), (second, own) in zip(sends, keeps)]
    mine = scattered(parts)
    mine = (mine + swap(mine, "wa", MASKS[0][0][4])[:, ::-1]) * pw_factor

    chunks = gathered_chunks(mine)
    operands = (place, weights, freqs, energy_val, energy_cond, orbit_val, orbit_cond, chunks)
    pair = pair_sums(((0, (0,)), (1, (0,))), *operands, [], 1)
    pair = pair_sums(((0, (1, 2)), (1, (1, 2))), *operands, pair, 1)
    pair = pair_sums(((0, (3,)),), *operands, pair, 1)
    keep, send = pair_sums(((1, (3,)),), *operands, pair, 2)
    pair = keep + swap(send, "ka", 1)
    total = wing_sums(place, everyone(pair, "wa"), zeta)
    total = total + swap(total, "ka", 1)
    total = total + swap(total, "ka", 2)
    return pl.pallas_call(
        functools.partial(final_kernel, float(2 * ways)),
        out_shape=[
            jax.ShapeDtypeStruct((3, nfreq, slab_rows), F32),
            jax.ShapeDtypeStruct((3, nfreq), F32),
        ],
        in_specs=[VMEM] * 2,
        out_specs=[VMEM] * 2,
        compiler_params=pltpu.CompilerParams(vmem_limit_bytes=4 << 20),
        name="final",
    )(total, swap(total, "ka", 6))


def solution(mesh):
    return jax.shard_map(
        local,
        mesh=mesh,
        in_specs=(
            P("ka", None, "wa"),
            P("ka", None, "wa"),
            P(None, "wa"),
            P("ka", None),
            P("ka", None),
            P("ka", None, "wa"),
            P("ka", None, "wa"),
            P("wa", None),
            P(),
            P("ka"),
        ),
        out_specs=(P(None, None, "wa"), P()),
        check_vma=False,
    )
```

```python
import functools

import jax
import jax.numpy as jnp
from jax import lax
from jax.experimental import pallas as pl
from jax.experimental.pallas import tpu as pltpu
from jax.sharding import PartitionSpec as P

MASKS = (((8, 24, 1, 3, 4), (1, 3, 8, 24, 4)), ((24, 8, 1, 3, 4), (3, 1, 8, 24, 4)))
CB, VB = 4, 8
F32, BF16 = jnp.float32, jnp.bfloat16
VMEM, SMEM = pl.BlockSpec(memory_space=pltpu.VMEM), pl.BlockSpec(memory_space=pltpu.SMEM)

def code_of(place, kpoint):
    index, core = place[0], place[1]
    x, z, y = index >> 3, (index >> 2) & 1, index & 3

    first, second = x + (y - x) * core, y + (x - y) * core
    one, two = (first ^ (first >> 1)) & 1, first >> 1
    quarter = one << 1 | two if kpoint == 0 else two << 1 | one
    return quarter, ((second ^ (second >> 1)) & 1) << 2 | (second >> 1) << 1 | z


def swap(value, axis, mask):
    return lax.ppermute(value, axis, [(i, i ^ mask) for i in range(lax.axis_size(axis))])


def cross(value, kpoint, *dims):
    groups, ways = lax.axis_size("ka"), lax.axis_size("wa")
    pairs = []
    for group in range(groups):
        mask = 0
        for dim in dims:
            mask ^= MASKS[kpoint][group & 1][dim]
        pairs += [(group * ways + i, group * ways + (i ^ mask)) for i in range(ways)]
    return lax.ppermute(value, ("ka", "wa"), pairs)


def everyone(value, axis):
    parts = lax.axis_size(axis)
    return lax.all_to_all(jnp.broadcast_to(value[None], (parts,) + value.shape), axis, 0, 0)


def gathered_chunks(kpoint, partial, factor):
    own, second, first, both = partial
    second = second + cross(both, kpoint, 0)
    one, two = cross(first, kpoint, 0), cross(second, kpoint, 1)

    def summed(place):
        lines = slice(2 * place, 2 * place + 2)
        return (own[lines] + one[lines]) + two[lines]

    held = (summed(0) + cross(summed(2), kpoint, 2)) + (
        cross(summed(1), kpoint, 3) + cross(summed(3), kpoint, 2, 3)
    )
    held = (held + cross(held, kpoint, 4)[::-1]) * factor
    others = [cross(held, kpoint, *dims) for dims in ((3,), (2,), (2, 3))]
    held = jnp.concatenate([held] + others)
    first, second = cross(held, kpoint, 0), cross(held, kpoint, 1)
    return held, second, first, cross(first, kpoint, 1)


def momentum_kernel(kpoint, quarters, place_ref, val_ref, miller_ref, cond_ref, *refs):
    outs, weighted = refs[:-1], refs[-1]
    nval = val_ref.shape[1]
    rows, cols = outs[0].shape[2:]
    me_c, me_v = code_of(place_ref, kpoint)
    for place in range(VB):
        source = pl.multiple_of((place ^ me_v) * rows, rows)
        block = val_ref[kpoint, pl.ds(source, rows), :].astype(F32)
        for axis in range(3):
            factor = miller_ref[axis : axis + 1, :].astype(F32)
            weighted[axis * nval + place * rows : axis * nval + (place + 1) * rows, :] = (
                block * factor
            ).astype(BF16)
    for quarter, out in zip(quarters, outs):
        start = pl.multiple_of((quarter ^ me_c) * cols, cols)
        result = lax.dot_general(
            weighted[...],
            cond_ref[kpoint, pl.ds(start, cols), :],
            (((1,), (1,)), ((), ())),
            preferred_element_type=F32,
        )
        for eighth in range(VB):
            for axis in range(3):
                start = axis * nval + eighth * rows
                out[eighth, axis] = result[start : start + rows]


def partial_momentum(kpoint, quarters, place, coeff_val, miller, coeff_cond):
    _, nval, depth = coeff_val.shape
    ncond = coeff_cond.shape[1]
    count = len(quarters)
    return pl.pallas_call(
        functools.partial(momentum_kernel, kpoint, quarters),
        out_shape=[jax.ShapeDtypeStruct((VB, 3, nval // VB, ncond // CB), F32)] * count,
        in_specs=[SMEM, VMEM, VMEM, VMEM],
        out_specs=[VMEM] * count,
        scratch_shapes=[pltpu.VMEM((3 * nval, depth), BF16)],
        cost_estimate=pl.CostEstimate(
            flops=2 * 3 * nval * ncond * depth * count // CB,
            bytes_accessed=(2 * nval + 2 * ncond * count // CB) * depth + 12 * nval * ncond * count // CB,
            transcendentals=0,
        ),
        compiler_params=pltpu.CompilerParams(vmem_limit_bytes=24 << 20),
        name="partial_momentum",
    )(place, coeff_val, miller, coeff_cond)


def pair_kernel(groups, place_ref, weight_ref, freq_ref, energy_val, energy_cond, orbit_val, orbit_cond, *refs):
    _, nval, points = orbit_val.shape
    ncond = orbit_cond.shape[1]
    nfreq = freq_ref.shape[0]
    count = sum(len(quarters) for _, quarters in groups)
    chunks, refs = refs[:count], refs[count:]
    begins = groups[0][1][0] == 0
    before, refs = (None, refs) if begins else (refs[0], refs[1:])
    outs, (total, amplitude, level, orbits, weight) = refs[:-5], refs[-5:]
    rows, cols = chunks[0].shape[2:]
    scale = float(nval * ncond) ** (-0.5)
    tops = 3 * nfreq
    for spot, (k, quarters) in enumerate(groups):
        mine, chunks = chunks[: len(quarters)], chunks[len(quarters) :]
        depth = len(quarters) * cols
        me_c, me_v = code_of(place_ref, k)
        level[spot] = jnp.transpose(jnp.broadcast_to(energy_val[k : k + 1, :], (nval, nval)))
        top = []
        for part, quarter in enumerate(quarters):
            start = pl.multiple_of((quarter ^ me_c) * cols, cols)
            top.append(energy_cond[k : k + 1, pl.ds(start, cols)])
            orbits[spot, part * cols : (part + 1) * cols, :] = orbit_cond[k, pl.ds(start, cols), :]

        def bottom_of(where, spot=spot):
            return jnp.concatenate([level[spot, where, :]] * (cols // nval), axis=1)

        def factors_of(gap):
            square = gap * gap
            return [4.0 / (square + freq_ref[w] * freq_ref[w]) for w in range(nfreq)]

        def eighth(place, carry, k=k, spot=spot, me_v=me_v, top=top, mine=mine, bottom_of=bottom_of):
            here = pl.ds(pl.multiple_of(place * rows, rows), rows)
            there = pl.ds(pl.multiple_of((place ^ me_v) * rows, rows), rows)
            weight[spot, here, :] = orbit_val[k, there, :].astype(F32) * (weight_ref[k] * scale)
            bottom = bottom_of(there)
            for part, chunk in enumerate(mine):
                factors = factors_of(top[part] - bottom)
                for axis in range(3):
                    momentum = chunk[place, axis]
                    for w in range(nfreq):
                        start = pl.multiple_of((axis * nfreq + w) * nval + place * rows, rows)
                        amplitude[spot, pl.ds(start, rows), part * cols : (part + 1) * cols] = (
                            momentum * factors[w]
                        ).astype(BF16)
            return carry

        lax.fori_loop(0, VB, eighth, 0, unroll=2)
        for axis in range(3):
            start = axis * nfreq * nval
            expanded = jnp.dot(
                amplitude[spot, start : start + nfreq * nval, :depth],
                orbits[spot, :depth, :],
                preferred_element_type=F32,
            )
            for w in range(nfreq):
                row = slice(axis * nfreq + w, axis * nfreq + w + 1)
                value = jnp.sum(expanded[w * nval : (w + 1) * nval] * weight[spot], axis=0, keepdims=True)
                if spot > 0:
                    value = value + total[row, :]
                elif not begins:
                    value = value + before[row, :]
                total[row, :] = value

        if begins:
            bottom = bottom_of(pl.ds(pl.multiple_of(me_v * rows, rows), rows))
            gap = top[0] - bottom
            ratios = [factor / gap for factor in factors_of(gap)]
            for axis in range(3):
                square = mine[0][0, axis] * mine[0][0, axis]
                row = slice(tops + axis, tops + axis + 1)
                for w in range(nfreq):
                    value = jnp.sum(square * ratios[w], axis=0, keepdims=True)
                    value = (value[:, :nval] + value[:, nval:]) * (weight_ref[k] / float(nval * ncond))
                    lanes = slice(w * nval, (w + 1) * nval)
                    total[row, lanes] = value + total[row, lanes] if spot else value
            row = slice(tops + 3, tops + 4)
            value = jnp.full((1, points), weight_ref[k], F32)
            total[row, :] = value + total[row, :] if spot else value
    if not begins:
        total[tops:, :] = before[tops:, :]
    if len(outs) == 2:
        keep, send = outs
        across = points // 2
        keep[...] = total[:, pl.ds(pl.multiple_of(place_ref[1] * across, across), across)]
        send[...] = total[:, pl.ds(pl.multiple_of((1 - place_ref[1]) * across, across), across)]
    else:
        outs[0][...] = total[...]


def pair_sums(groups, place, weights, freqs, energy_val, energy_cond, orbit_val, orbit_cond, chunks, before, parts):
    _, nval, points = orbit_val.shape
    ncond = orbit_cond.shape[1]
    nfreq = freqs.shape[0]
    height = 3 * nfreq + 4
    depth = ncond // CB * max(len(quarters) for _, quarters in groups)
    count = len(groups)
    operands = [energy_val, energy_cond, orbit_val, orbit_cond]
    operands += [chunks[k][quarter] for k, quarters in groups for quarter in quarters]
    operands += before
    return list(
        pl.pallas_call(
            functools.partial(pair_kernel, groups),
            out_shape=[jax.ShapeDtypeStruct((height, points // parts), F32)] * parts,
            in_specs=[SMEM] * 3 + [VMEM] * len(operands),
            out_specs=[VMEM] * parts,
            scratch_shapes=[
                pltpu.VMEM((height, points), F32),
                pltpu.VMEM((count, 3 * nfreq * nval, depth), BF16),
                pltpu.VMEM((count, nval, nval), F32),
                pltpu.VMEM((count, depth, points), BF16),
                pltpu.VMEM((count, nval, points), F32),
            ],
            cost_estimate=pl.CostEstimate(
                flops=count * 2 * 3 * nfreq * nval * depth * points,
                bytes_accessed=count * (12 * nval * depth + 4 * depth * points),
                transcendentals=0,
            ),
            compiler_params=pltpu.CompilerParams(vmem_limit_bytes=20 << 20),
            name="pair_sums",
        )(place, weights, freqs, *operands)
    )


def wing_kernel(place_ref, gathered, zeta, out):
    ways, height, points = gathered.shape
    slab_rows = zeta.shape[0]
    tops = height - 4
    total = jnp.zeros((3 * height, slab_rows), F32)
    last = jnp.zeros((4, points), F32)
    for device in range(ways):
        value = gathered[device]
        last = last + value[tops:]
        pieces = []
        for _ in range(3):
            rounded = value.astype(BF16)
            pieces.append(rounded)
            value = value - rounded.astype(F32)
        start = pl.multiple_of((2 * device + place_ref[1]) * points, points)
        total = total + lax.dot_general(
            jnp.concatenate(pieces, axis=0),
            zeta[:, pl.ds(start, points)],
            (((1,), (1,)), ((), ())),
            preferred_element_type=F32,
        )
    total = total[:height] + total[height : 2 * height] + total[2 * height :]
    out[:tops] = total[:tops]
    lane = lax.broadcasted_iota(jnp.int32, (3, slab_rows), 1)
    across = points // 2
    head = jnp.zeros((3, slab_rows), F32)
    for tile in range(2):
        value = jnp.sum(last[:3, tile * across : (tile + 1) * across], axis=1, keepdims=True)
        head = jnp.where(lane == 2 * place_ref[1] + tile, value, head)
    out[tops : tops + 3] = head
    out[tops + 3 :] = last[3:, :slab_rows]


def wing_sums(place, gathered, zeta):
    ways, height, points = gathered.shape
    slab_rows = zeta.shape[0]
    return pl.pallas_call(
        wing_kernel,
        out_shape=jax.ShapeDtypeStruct((height, slab_rows), F32),
        in_specs=[SMEM, VMEM, VMEM],
        out_specs=VMEM,
        cost_estimate=pl.CostEstimate(
            flops=6 * height * slab_rows * ways * points,
            bytes_accessed=4 * slab_rows * ways * points + 4 * height * ways * points,
            transcendentals=0,
        ),
        compiler_params=pltpu.CompilerParams(vmem_limit_bytes=20 << 20),
        name="wing_sums",
    )(place, gathered, zeta)


def final_kernel(copies, one, two, wing, head):
    total = one[...] + two[...]
    tops = total.shape[0] - 4
    nfreq = wing.shape[1]
    scale = copies / total[tops + 3 :]
    for axis in range(3):
        wing[axis] = total[axis * nfreq : (axis + 1) * nfreq] * scale
    head[...] = total[tops : tops + 3, :nfreq] * scale[:, :nfreq]


def local(
    coeff_val,
    coeff_cond,
    miller,
    energy_val,
    energy_cond,
    orbit_val,
    orbit_cond,
    zeta,
    freqs,
    kweight,
):
    kcount, nval, npw_dev = coeff_val.shape
    nfreq = freqs.shape[0]
    slab_rows = zeta.shape[0]
    ways = lax.axis_size("wa")
    pw_factor = float(npw_dev * ways) ** (-0.5)
    weights = kweight.astype(F32)
    place = jnp.stack([lax.axis_index("wa"), lax.axis_index("ka") & 1]).astype(jnp.int32)

    operands = (place, coeff_val, miller, coeff_cond)
    sends = [partial_momentum(k, (3, 2), *operands) for k in range(kcount)]
    keeps = [partial_momentum(k, (1, 0), *operands) for k in range(kcount)]
    parts = [(own, second, first, both) for (both, first), (second, own) in zip(sends, keeps)]
    chunks = [gathered_chunks(k, parts[k], pw_factor) for k in range(kcount)]
    operands = (place, weights, freqs, energy_val, energy_cond, orbit_val, orbit_cond, chunks)
    pair = pair_sums(((0, (0,)), (1, (0,))), *operands, [], 1)
    pair = pair_sums(((0, (1, 2)), (1, (1, 2))), *operands, pair, 1)
    pair = pair_sums(((0, (3,)),), *operands, pair, 1)
    keep, send = pair_sums(((1, (3,)),), *operands, pair, 2)
    pair = keep + swap(send, "ka", 1)
    total = wing_sums(place, everyone(pair, "wa"), zeta)
    total = total + swap(total, "ka", 1)
    total = total + swap(total, "ka", 2)
    return pl.pallas_call(
        functools.partial(final_kernel, float(2 * ways)),
        out_shape=[
            jax.ShapeDtypeStruct((3, nfreq, slab_rows), F32),
            jax.ShapeDtypeStruct((3, nfreq), F32),
        ],
        in_specs=[VMEM] * 2,
        out_specs=[VMEM] * 2,
        compiler_params=pltpu.CompilerParams(vmem_limit_bytes=4 << 20),
        name="final",
    )(total, swap(total, "ka", 6))


def solution(mesh):
    return jax.shard_map(
        local,
        mesh=mesh,
        in_specs=(
            P("ka", None, "wa"),
            P("ka", None, "wa"),
            P(None, "wa"),
            P("ka", None),
            P("ka", None),
            P("ka", None, "wa"),
            P("ka", None, "wa"),
            P("wa", None),
            P(),
            P("ka"),
        ),
        out_specs=(P(None, None, "wa"), P()),
        check_vma=False,
    )
```

```python
import functools

import jax
import jax.numpy as jnp
from jax import lax
from jax.experimental import pallas as pl
from jax.experimental.pallas import tpu as pltpu
from jax.sharding import PartitionSpec as P

MASKS = (((8, 24, 1, 3, 4), (24, 8, 1, 3, 4)), ((1, 3, 8, 24, 4), (3, 1, 8, 24, 4)))
CB, VB = 4, 8
F32, BF16 = jnp.float32, jnp.bfloat16
VMEM, SMEM = pl.BlockSpec(memory_space=pltpu.VMEM), pl.BlockSpec(memory_space=pltpu.SMEM)

def code_of(place, kpoint):
    index, core = place[0], place[1]
    x, z, y = index >> 3, (index >> 2) & 1, index & 3

    first, second = (x, y) if kpoint == 0 else (y, x)
    one, two = (first ^ (first >> 1)) & 1, first >> 1
    quarter = (one << 1 | two) + ((two << 1 | one) - (one << 1 | two)) * core
    return quarter, ((second ^ (second >> 1)) & 1) << 2 | (second >> 1) << 1 | z


def swap(value, axis, mask):
    return lax.ppermute(value, axis, [(i, i ^ mask) for i in range(lax.axis_size(axis))])


def cross(value, kpoint, *dims):
    groups, ways = lax.axis_size("ka"), lax.axis_size("wa")
    pairs = []
    for group in range(groups):
        mask = 0
        for dim in dims:
            mask ^= MASKS[kpoint][group & 1][dim]
        pairs += [(group * ways + i, group * ways + (i ^ mask)) for i in range(ways)]
    return lax.ppermute(value, ("ka", "wa"), pairs)


def everyone(value, axis):
    parts = lax.axis_size(axis)
    return lax.all_to_all(jnp.broadcast_to(value[None], (parts,) + value.shape), axis, 0, 0)


def gathered_chunks(kpoint, partial, factor):
    own, second, first, both = partial
    second = second + cross(both, kpoint, 0)
    one, two = cross(first, kpoint, 0), cross(second, kpoint, 1)

    def summed(place):
        lines = slice(2 * place, 2 * place + 2)
        return (own[lines] + one[lines]) + two[lines]

    held = (summed(0) + cross(summed(2), kpoint, 2)) + (
        cross(summed(1), kpoint, 3) + cross(summed(3), kpoint, 2, 3)
    )
    held = (held + cross(held, kpoint, 4)[::-1]) * factor
    others = [cross(held, kpoint, *dims) for dims in ((3,), (2,), (2, 3))]
    held = jnp.concatenate([held] + others)
    first, second = cross(held, kpoint, 0), cross(held, kpoint, 1)
    return held, second, first


def momentum_kernel(kpoint, quarters, place_ref, val_ref, miller_ref, cond_ref, *refs):
    outs, weighted = refs[:-1], refs[-1]
    nval = val_ref.shape[1]
    rows, cols = outs[0].shape[2:]
    me_c, me_v = code_of(place_ref, kpoint)
    for place in range(VB):
        source = pl.multiple_of((place ^ me_v) * rows, rows)
        block = val_ref[kpoint, pl.ds(source, rows), :].astype(F32)
        for axis in range(3):
            factor = miller_ref[axis : axis + 1, :].astype(F32)
            weighted[axis * nval + place * rows : axis * nval + (place + 1) * rows, :] = (
                block * factor
            ).astype(BF16)
    for quarter, out in zip(quarters, outs):
        start = pl.multiple_of((quarter ^ me_c) * cols, cols)
        result = lax.dot_general(
            weighted[...],
            cond_ref[kpoint, pl.ds(start, cols), :],
            (((1,), (1,)), ((), ())),
            preferred_element_type=F32,
        )
        for eighth in range(VB):
            for axis in range(3):
                start = axis * nval + eighth * rows
                out[eighth, axis] = result[start : start + rows]


def partial_momentum(kpoint, quarters, place, coeff_val, miller, coeff_cond):
    _, nval, depth = coeff_val.shape
    ncond = coeff_cond.shape[1]
    count = len(quarters)
    return pl.pallas_call(
        functools.partial(momentum_kernel, kpoint, quarters),
        out_shape=[jax.ShapeDtypeStruct((VB, 3, nval // VB, ncond // CB), F32)] * count,
        in_specs=[SMEM, VMEM, VMEM, VMEM],
        out_specs=[VMEM] * count,
        scratch_shapes=[pltpu.VMEM((3 * nval, depth), BF16)],
        cost_estimate=pl.CostEstimate(
            flops=2 * 3 * nval * ncond * depth * count // CB,
            bytes_accessed=(2 * nval + 2 * ncond * count // CB) * depth + 12 * nval * ncond * count // CB,
            transcendentals=0,
        ),
        compiler_params=pltpu.CompilerParams(vmem_limit_bytes=24 << 20),
        name="partial_momentum",
    )(place, coeff_val, miller, coeff_cond)


def pair_kernel(groups, place_ref, weight_ref, freq_ref, energy_val, energy_cond, orbit_val, orbit_cond, *refs):
    _, nval, points = orbit_val.shape
    ncond = orbit_cond.shape[1]
    nfreq = freq_ref.shape[0]
    count = sum(len(quarters) for _, quarters in groups)
    chunks, refs = refs[:count], refs[count:]
    begins = groups[0] == (0, (0,))
    before, refs = (None, refs) if begins else (refs[0], refs[1:])
    outs, (total, amplitude, level, orbits, weight) = refs[:-5], refs[-5:]
    rows, cols = chunks[0].shape[2:]
    scale = float(nval * ncond) ** (-0.5)
    tops = 3 * nfreq
    for spot, (k, quarters) in enumerate(groups):
        mine, chunks = chunks[: len(quarters)], chunks[len(quarters) :]
        depth = len(quarters) * cols
        me_c, me_v = code_of(place_ref, k)
        level[spot] = jnp.transpose(jnp.broadcast_to(energy_val[k : k + 1, :], (nval, nval)))
        top = []
        for part, quarter in enumerate(quarters):
            start = pl.multiple_of((quarter ^ me_c) * cols, cols)
            top.append(energy_cond[k : k + 1, pl.ds(start, cols)])
            orbits[spot, part * cols : (part + 1) * cols, :] = orbit_cond[k, pl.ds(start, cols), :]

        def bottom_of(where, spot=spot):
            return jnp.concatenate([level[spot, where, :]] * (cols // nval), axis=1)

        def factors_of(gap):
            square = gap * gap
            return [4.0 / (square + freq_ref[w] * freq_ref[w]) for w in range(nfreq)]

        def eighth(place, carry, k=k, spot=spot, me_v=me_v, top=top, mine=mine, bottom_of=bottom_of):
            here = pl.ds(pl.multiple_of(place * rows, rows), rows)
            there = pl.ds(pl.multiple_of((place ^ me_v) * rows, rows), rows)
            weight[spot, here, :] = orbit_val[k, there, :].astype(F32) * (weight_ref[k] * scale)
            bottom = bottom_of(there)
            for part, chunk in enumerate(mine):
                factors = factors_of(top[part] - bottom)
                for axis in range(3):
                    momentum = chunk[place, axis]
                    for w in range(nfreq):
                        start = pl.multiple_of((axis * nfreq + w) * nval + place * rows, rows)
                        amplitude[spot, pl.ds(start, rows), part * cols : (part + 1) * cols] = (
                            momentum * factors[w]
                        ).astype(BF16)
            return carry

        lax.fori_loop(0, VB, eighth, 0, unroll=2)
        for axis in range(3):
            start = axis * nfreq * nval
            expanded = jnp.dot(
                amplitude[spot, start : start + nfreq * nval, :depth],
                orbits[spot, :depth, :],
                preferred_element_type=F32,
            )
            for w in range(nfreq):
                row = slice(axis * nfreq + w, axis * nfreq + w + 1)
                value = jnp.sum(expanded[w * nval : (w + 1) * nval] * weight[spot], axis=0, keepdims=True)
                if spot > 0:
                    value = value + total[row, :]
                elif not begins:
                    value = value + before[row, :]
                total[row, :] = value

        if quarters[0] == 0:
            bottom = bottom_of(pl.ds(pl.multiple_of(me_v * rows, rows), rows))
            gap = top[0] - bottom
            ratios = [factor / gap for factor in factors_of(gap)]
            for axis in range(3):
                square = mine[0][0, axis] * mine[0][0, axis]
                row = slice(tops + axis, tops + axis + 1)
                for w in range(nfreq):
                    value = jnp.sum(square * ratios[w], axis=0, keepdims=True)
                    value = (value[:, :nval] + value[:, nval:]) * (weight_ref[k] / float(nval * ncond))
                    lanes = slice(w * nval, (w + 1) * nval)
                    total[row, lanes] = value if begins else value + before[row, lanes]
            row = slice(tops + 3, tops + 4)
            value = jnp.full((1, points), weight_ref[k], F32)
            total[row, :] = value if begins else value + before[row, :]
    if groups[0][1][0] != 0:
        total[tops:, :] = before[tops:, :]
    if len(outs) == 2:
        keep, send = outs
        across = points // 2
        keep[...] = total[:, pl.ds(pl.multiple_of(place_ref[1] * across, across), across)]
        send[...] = total[:, pl.ds(pl.multiple_of((1 - place_ref[1]) * across, across), across)]
    else:
        outs[0][...] = total[...]


def pair_sums(groups, place, weights, freqs, energy_val, energy_cond, orbit_val, orbit_cond, chunks, before, parts):
    _, nval, points = orbit_val.shape
    ncond = orbit_cond.shape[1]
    nfreq = freqs.shape[0]
    height = 3 * nfreq + 4
    depth = ncond // CB * max(len(quarters) for _, quarters in groups)
    count = len(groups)
    operands = [energy_val, energy_cond, orbit_val, orbit_cond]
    operands += [chunks[k][quarter] for k, quarters in groups for quarter in quarters]
    operands += before
    return list(
        pl.pallas_call(
            functools.partial(pair_kernel, groups),
            out_shape=[jax.ShapeDtypeStruct((height, points // parts), F32)] * parts,
            in_specs=[SMEM] * 3 + [VMEM] * len(operands),
            out_specs=[VMEM] * parts,
            scratch_shapes=[
                pltpu.VMEM((height, points), F32),
                pltpu.VMEM((count, 3 * nfreq * nval, depth), BF16),
                pltpu.VMEM((count, nval, nval), F32),
                pltpu.VMEM((count, depth, points), BF16),
                pltpu.VMEM((count, nval, points), F32),
            ],
            cost_estimate=pl.CostEstimate(
                flops=count * 2 * 3 * nfreq * nval * depth * points,
                bytes_accessed=count * (12 * nval * depth + 4 * depth * points),
                transcendentals=0,
            ),
            compiler_params=pltpu.CompilerParams(vmem_limit_bytes=20 << 20),
            name="pair_sums",
        )(place, weights, freqs, *operands)
    )


def wing_kernel(place_ref, gathered, zeta, out):
    ways, height, points = gathered.shape
    slab_rows = zeta.shape[0]
    tops = height - 4
    total = jnp.zeros((3 * height, slab_rows), F32)
    last = jnp.zeros((4, points), F32)
    for device in range(ways):
        value = gathered[device]
        last = last + value[tops:]
        pieces = []
        for _ in range(3):
            rounded = value.astype(BF16)
            pieces.append(rounded)
            value = value - rounded.astype(F32)
        start = pl.multiple_of((2 * device + place_ref[1]) * points, points)
        total = total + lax.dot_general(
            jnp.concatenate(pieces, axis=0),
            zeta[:, pl.ds(start, points)],
            (((1,), (1,)), ((), ())),
            preferred_element_type=F32,
        )
    total = total[:height] + total[height : 2 * height] + total[2 * height :]
    out[:tops] = total[:tops]
    lane = lax.broadcasted_iota(jnp.int32, (3, slab_rows), 1)
    across = points // 2
    head = jnp.zeros((3, slab_rows), F32)
    for tile in range(2):
        value = jnp.sum(last[:3, tile * across : (tile + 1) * across], axis=1, keepdims=True)
        head = jnp.where(lane == 2 * place_ref[1] + tile, value, head)
    out[tops : tops + 3] = head
    out[tops + 3 :] = last[3:, :slab_rows]


def wing_sums(place, gathered, zeta):
    ways, height, points = gathered.shape
    slab_rows = zeta.shape[0]
    return pl.pallas_call(
        wing_kernel,
        out_shape=jax.ShapeDtypeStruct((height, slab_rows), F32),
        in_specs=[SMEM, VMEM, VMEM],
        out_specs=VMEM,
        cost_estimate=pl.CostEstimate(
            flops=6 * height * slab_rows * ways * points,
            bytes_accessed=4 * slab_rows * ways * points + 4 * height * ways * points,
            transcendentals=0,
        ),
        compiler_params=pltpu.CompilerParams(vmem_limit_bytes=20 << 20),
        name="wing_sums",
    )(place, gathered, zeta)


def final_kernel(copies, one, two, wing, head):
    total = one[...] + two[...]
    tops = total.shape[0] - 4
    nfreq = wing.shape[1]
    scale = copies / total[tops + 3 :]
    for axis in range(3):
        wing[axis] = total[axis * nfreq : (axis + 1) * nfreq] * scale
    head[...] = total[tops : tops + 3, :nfreq] * scale[:, :nfreq]


def local(
    coeff_val,
    coeff_cond,
    miller,
    energy_val,
    energy_cond,
    orbit_val,
    orbit_cond,
    zeta,
    freqs,
    kweight,
):
    kcount, nval, npw_dev = coeff_val.shape
    nfreq = freqs.shape[0]
    slab_rows = zeta.shape[0]
    ways = lax.axis_size("wa")
    pw_factor = float(npw_dev * ways) ** (-0.5)
    weights = kweight.astype(F32)
    place = jnp.stack([lax.axis_index("wa"), lax.axis_index("ka") & 1]).astype(jnp.int32)

    operands = (place, coeff_val, miller, coeff_cond)
    sends = [partial_momentum(k, (3, 2), *operands) for k in range(kcount)]
    keeps = [partial_momentum(k, (1, 0), *operands) for k in range(kcount)]
    parts = [(own, second, first, both) for (both, first), (second, own) in zip(sends, keeps)]
    chunks = [gathered_chunks(k, parts[k], pw_factor) for k in range(kcount)]
    operands = (place, weights, freqs, energy_val, energy_cond, orbit_val, orbit_cond)
    pair = []
    for k in range(kcount):
        own, second, first = chunks[k]
        pair = pair_sums(((k, (0,)),), *operands, {k: (own,)}, pair, 1)
        first, pair = lax.optimization_barrier((first, pair))
        chunks[k] = (own, second, first, cross(first, k, 1))
    pair = pair_sums(((0, (1, 2)), (1, (1, 2))), *operands, chunks, pair, 1)
    pair = pair_sums(((0, (3,)),), *operands, chunks, pair, 1)
    keep, send = pair_sums(((1, (3,)),), *operands, chunks, pair, 2)
    pair = keep + swap(send, "ka", 1)
    total = wing_sums(place, everyone(pair, "wa"), zeta)
    total = total + swap(total, "ka", 1)
    total = total + swap(total, "ka", 2)
    return pl.pallas_call(
        functools.partial(final_kernel, float(2 * ways)),
        out_shape=[
            jax.ShapeDtypeStruct((3, nfreq, slab_rows), F32),
            jax.ShapeDtypeStruct((3, nfreq), F32),
        ],
        in_specs=[VMEM] * 2,
        out_specs=[VMEM] * 2,
        compiler_params=pltpu.CompilerParams(vmem_limit_bytes=4 << 20),
        name="final",
    )(total, swap(total, "ka", 6))


def solution(mesh):
    return jax.shard_map(
        local,
        mesh=mesh,
        in_specs=(
            P("ka", None, "wa"),
            P("ka", None, "wa"),
            P(None, "wa"),
            P("ka", None),
            P("ka", None),
            P("ka", None, "wa"),
            P("ka", None, "wa"),
            P("wa", None),
            P(),
            P("ka"),
        ),
        out_specs=(P(None, None, "wa"), P()),
        check_vma=False,
    )
```

```python
import functools

import jax
import jax.numpy as jnp
from jax import lax
from jax.experimental import pallas as pl
from jax.experimental.pallas import tpu as pltpu
from jax.sharding import PartitionSpec as P

MASKS = (((8, 24, 1, 3, 4), (24, 8, 1, 3, 4)), ((1, 3, 8, 24, 4), (3, 1, 8, 24, 4)))
CB, VB = 4, 8
F32, BF16 = jnp.float32, jnp.bfloat16
VMEM, SMEM = pl.BlockSpec(memory_space=pltpu.VMEM), pl.BlockSpec(memory_space=pltpu.SMEM)

def code_of(place, kpoint):
    index, core = place[0], place[1]
    x, z, y = index >> 3, (index >> 2) & 1, index & 3

    first, second = (x, y) if kpoint == 0 else (y, x)
    one, two = (first ^ (first >> 1)) & 1, first >> 1
    quarter = (one << 1 | two) + ((two << 1 | one) - (one << 1 | two)) * core
    return quarter, ((second ^ (second >> 1)) & 1) << 2 | (second >> 1) << 1 | z


def swap(value, axis, mask):
    return lax.ppermute(value, axis, [(i, i ^ mask) for i in range(lax.axis_size(axis))])


def cross(value, kpoint, *dims):
    groups, ways = lax.axis_size("ka"), lax.axis_size("wa")
    pairs = []
    for group in range(groups):
        mask = 0
        for dim in dims:
            mask ^= MASKS[kpoint][group & 1][dim]
        pairs += [(group * ways + i, group * ways + (i ^ mask)) for i in range(ways)]
    return lax.ppermute(value, ("ka", "wa"), pairs)


def everyone(value, axis):
    parts = lax.axis_size(axis)
    return lax.all_to_all(jnp.broadcast_to(value[None], (parts,) + value.shape), axis, 0, 0)


def gathered_chunks(kpoint, partial, factor):
    own, second, first, both = partial
    second = second + cross(both, kpoint, 0)
    one, two = cross(first, kpoint, 0), cross(second, kpoint, 1)

    def summed(place):
        lines = slice(2 * place, 2 * place + 2)
        return (own[lines] + one[lines]) + two[lines]

    held = (summed(0) + cross(summed(2), kpoint, 2)) + (
        cross(summed(1), kpoint, 3) + cross(summed(3), kpoint, 2, 3)
    )
    held = (held + cross(held, kpoint, 4)[::-1]) * factor
    others = [cross(held, kpoint, *dims) for dims in ((3,), (2,), (2, 3))]
    held = jnp.concatenate([held] + others)
    first, second = cross(held, kpoint, 0), cross(held, kpoint, 1)
    return held, second, first


def weight_kernel(place_ref, val_ref, miller_ref, out):
    kcount, nval, _ = val_ref.shape
    rows = nval // VB
    factors = [miller_ref[axis : axis + 1, :].astype(F32) for axis in range(3)]
    for k in range(kcount):
        _, me_v = code_of(place_ref, k)
        for place in range(VB):
            source = pl.multiple_of((place ^ me_v) * rows, rows)
            block = val_ref[k, pl.ds(source, rows), :].astype(F32)
            for axis in range(3):
                start = axis * nval + place * rows
                out[k, start : start + rows, :] = (block * factors[axis]).astype(BF16)


def weighted_values(place, coeff_val, miller):
    kcount, nval, depth = coeff_val.shape
    return pl.pallas_call(
        weight_kernel,
        out_shape=jax.ShapeDtypeStruct((kcount, 3 * nval, depth), BF16),
        in_specs=[SMEM, VMEM, VMEM],
        out_specs=VMEM,
        cost_estimate=pl.CostEstimate(
            flops=3 * kcount * nval * depth, bytes_accessed=8 * kcount * nval * depth, transcendentals=0
        ),
        compiler_params=pltpu.CompilerParams(vmem_limit_bytes=16 << 20),
        name="weighted_values",
    )(place, coeff_val, miller)


def momentum_kernel(kpoint, quarters, place_ref, weighted, cond_ref, *outs):
    nval = weighted.shape[1] // 3
    rows, cols = outs[0].shape[2:]
    me_c, _ = code_of(place_ref, kpoint)
    for quarter, out in zip(quarters, outs):
        start = pl.multiple_of((quarter ^ me_c) * cols, cols)
        result = lax.dot_general(
            weighted[kpoint],
            cond_ref[kpoint, pl.ds(start, cols), :],
            (((1,), (1,)), ((), ())),
            preferred_element_type=F32,
        )
        for eighth in range(VB):
            for axis in range(3):
                start = axis * nval + eighth * rows
                out[eighth, axis] = result[start : start + rows]


def partial_momentum(kpoint, quarters, place, weighted, coeff_cond):
    _, height, depth = weighted.shape
    ncond = coeff_cond.shape[1]
    count = len(quarters)
    return pl.pallas_call(
        functools.partial(momentum_kernel, kpoint, quarters),
        out_shape=[jax.ShapeDtypeStruct((VB, 3, height // 3 // VB, ncond // CB), F32)] * count,
        in_specs=[SMEM, VMEM, VMEM],
        out_specs=[VMEM] * count,
        cost_estimate=pl.CostEstimate(
            flops=2 * height * ncond * depth * count // CB,
            bytes_accessed=2 * (height + ncond * count // CB) * depth + 4 * height * ncond * count // CB,
            transcendentals=0,
        ),
        compiler_params=pltpu.CompilerParams(vmem_limit_bytes=24 << 20),
        name="partial_momentum",
    )(place, weighted, coeff_cond)


def pair_kernel(groups, place_ref, weight_ref, freq_ref, energy_val, energy_cond, orbit_val, orbit_cond, *refs):
    _, nval, points = orbit_val.shape
    ncond = orbit_cond.shape[1]
    nfreq = freq_ref.shape[0]
    count = sum(len(quarters) for _, quarters in groups)
    chunks, refs = refs[:count], refs[count:]
    begins = groups[0] == (0, (0,))
    before, refs = (None, refs) if begins else (refs[0], refs[1:])
    outs, (total, amplitude, level, orbits, weight) = refs[:-5], refs[-5:]
    rows, cols = chunks[0].shape[2:]
    scale = float(nval * ncond) ** (-0.5)
    tops = 3 * nfreq
    for spot, (k, quarters) in enumerate(groups):
        mine, chunks = chunks[: len(quarters)], chunks[len(quarters) :]
        depth = len(quarters) * cols
        me_c, me_v = code_of(place_ref, k)
        level[spot] = jnp.transpose(jnp.broadcast_to(energy_val[k : k + 1, :], (nval, nval)))
        top = []
        for part, quarter in enumerate(quarters):
            start = pl.multiple_of((quarter ^ me_c) * cols, cols)
            top.append(energy_cond[k : k + 1, pl.ds(start, cols)])
            orbits[spot, part * cols : (part + 1) * cols, :] = orbit_cond[k, pl.ds(start, cols), :]

        def bottom_of(where, spot=spot):
            return jnp.concatenate([level[spot, where, :]] * (cols // nval), axis=1)

        def factors_of(gap):
            square = gap * gap
            return [4.0 / (square + freq_ref[w] * freq_ref[w]) for w in range(nfreq)]

        def eighth(place, carry, k=k, spot=spot, me_v=me_v, top=top, mine=mine, bottom_of=bottom_of):
            here = pl.ds(pl.multiple_of(place * rows, rows), rows)
            there = pl.ds(pl.multiple_of((place ^ me_v) * rows, rows), rows)
            weight[spot, here, :] = orbit_val[k, there, :].astype(F32) * (weight_ref[k] * scale)
            bottom = bottom_of(there)
            for part, chunk in enumerate(mine):
                factors = factors_of(top[part] - bottom)
                for axis in range(3):
                    momentum = chunk[place, axis]
                    for w in range(nfreq):
                        start = pl.multiple_of((axis * nfreq + w) * nval + place * rows, rows)
                        amplitude[spot, pl.ds(start, rows), part * cols : (part + 1) * cols] = (
                            momentum * factors[w]
                        ).astype(BF16)
            return carry

        lax.fori_loop(0, VB, eighth, 0, unroll=2)
        for axis in range(3):
            start = axis * nfreq * nval
            expanded = jnp.dot(
                amplitude[spot, start : start + nfreq * nval, :depth],
                orbits[spot, :depth, :],
                preferred_element_type=F32,
            )
            for w in range(nfreq):
                row = slice(axis * nfreq + w, axis * nfreq + w + 1)
                value = jnp.sum(expanded[w * nval : (w + 1) * nval] * weight[spot], axis=0, keepdims=True)
                if spot > 0:
                    value = value + total[row, :]
                elif not begins:
                    value = value + before[row, :]
                total[row, :] = value

        if quarters[0] == 0:
            bottom = bottom_of(pl.ds(pl.multiple_of(me_v * rows, rows), rows))
            gap = top[0] - bottom
            ratios = [factor / gap for factor in factors_of(gap)]
            for axis in range(3):
                square = mine[0][0, axis] * mine[0][0, axis]
                row = slice(tops + axis, tops + axis + 1)
                for w in range(nfreq):
                    value = jnp.sum(square * ratios[w], axis=0, keepdims=True)
                    value = (value[:, :nval] + value[:, nval:]) * (weight_ref[k] / float(nval * ncond))
                    lanes = slice(w * nval, (w + 1) * nval)
                    total[row, lanes] = value if begins else value + before[row, lanes]
            row = slice(tops + 3, tops + 4)
            value = jnp.full((1, points), weight_ref[k], F32)
            total[row, :] = value if begins else value + before[row, :]
    if groups[0][1][0] != 0:
        total[tops:, :] = before[tops:, :]
    if len(outs) == 2:
        keep, send = outs
        across = points // 2
        keep[...] = total[:, pl.ds(pl.multiple_of(place_ref[1] * across, across), across)]
        send[...] = total[:, pl.ds(pl.multiple_of((1 - place_ref[1]) * across, across), across)]
    else:
        outs[0][...] = total[...]


def pair_sums(groups, place, weights, freqs, energy_val, energy_cond, orbit_val, orbit_cond, chunks, before, parts):
    _, nval, points = orbit_val.shape
    ncond = orbit_cond.shape[1]
    nfreq = freqs.shape[0]
    height = 3 * nfreq + 4
    depth = ncond // CB * max(len(quarters) for _, quarters in groups)
    count = len(groups)
    operands = [energy_val, energy_cond, orbit_val, orbit_cond]
    operands += [chunks[k][quarter] for k, quarters in groups for quarter in quarters]
    operands += before
    return list(
        pl.pallas_call(
            functools.partial(pair_kernel, groups),
            out_shape=[jax.ShapeDtypeStruct((height, points // parts), F32)] * parts,
            in_specs=[SMEM] * 3 + [VMEM] * len(operands),
            out_specs=[VMEM] * parts,
            scratch_shapes=[
                pltpu.VMEM((height, points), F32),
                pltpu.VMEM((count, 3 * nfreq * nval, depth), BF16),
                pltpu.VMEM((count, nval, nval), F32),
                pltpu.VMEM((count, depth, points), BF16),
                pltpu.VMEM((count, nval, points), F32),
            ],
            cost_estimate=pl.CostEstimate(
                flops=count * 2 * 3 * nfreq * nval * depth * points,
                bytes_accessed=count * (12 * nval * depth + 4 * depth * points),
                transcendentals=0,
            ),
            compiler_params=pltpu.CompilerParams(vmem_limit_bytes=20 << 20),
            name="pair_sums",
        )(place, weights, freqs, *operands)
    )


def wing_kernel(place_ref, gathered, zeta, out):
    ways, height, points = gathered.shape
    slab_rows = zeta.shape[0]
    tops = height - 4
    total = jnp.zeros((3 * height, slab_rows), F32)
    last = jnp.zeros((4, points), F32)
    for device in range(ways):
        value = gathered[device]
        last = last + value[tops:]
        pieces = []
        for _ in range(3):
            rounded = value.astype(BF16)
            pieces.append(rounded)
            value = value - rounded.astype(F32)
        start = pl.multiple_of((2 * device + place_ref[1]) * points, points)
        total = total + lax.dot_general(
            jnp.concatenate(pieces, axis=0),
            zeta[:, pl.ds(start, points)],
            (((1,), (1,)), ((), ())),
            preferred_element_type=F32,
        )
    total = total[:height] + total[height : 2 * height] + total[2 * height :]
    out[:tops] = total[:tops]
    lane = lax.broadcasted_iota(jnp.int32, (3, slab_rows), 1)
    across = points // 2
    head = jnp.zeros((3, slab_rows), F32)
    for tile in range(2):
        value = jnp.sum(last[:3, tile * across : (tile + 1) * across], axis=1, keepdims=True)
        head = jnp.where(lane == 2 * place_ref[1] + tile, value, head)
    out[tops : tops + 3] = head
    out[tops + 3 :] = last[3:, :slab_rows]


def wing_sums(place, gathered, zeta):
    ways, height, points = gathered.shape
    slab_rows = zeta.shape[0]
    return pl.pallas_call(
        wing_kernel,
        out_shape=jax.ShapeDtypeStruct((height, slab_rows), F32),
        in_specs=[SMEM, VMEM, VMEM],
        out_specs=VMEM,
        cost_estimate=pl.CostEstimate(
            flops=6 * height * slab_rows * ways * points,
            bytes_accessed=4 * slab_rows * ways * points + 4 * height * ways * points,
            transcendentals=0,
        ),
        compiler_params=pltpu.CompilerParams(vmem_limit_bytes=20 << 20),
        name="wing_sums",
    )(place, gathered, zeta)


def final_kernel(copies, one, two, wing, head):
    total = one[...] + two[...]
    tops = total.shape[0] - 4
    nfreq = wing.shape[1]
    scale = copies / total[tops + 3 :]
    for axis in range(3):
        wing[axis] = total[axis * nfreq : (axis + 1) * nfreq] * scale
    head[...] = total[tops : tops + 3, :nfreq] * scale[:, :nfreq]


def local(
    coeff_val,
    coeff_cond,
    miller,
    energy_val,
    energy_cond,
    orbit_val,
    orbit_cond,
    zeta,
    freqs,
    kweight,
):
    kcount, nval, npw_dev = coeff_val.shape
    nfreq = freqs.shape[0]
    slab_rows = zeta.shape[0]
    ways = lax.axis_size("wa")
    pw_factor = float(npw_dev * ways) ** (-0.5)
    weights = kweight.astype(F32)
    place = jnp.stack([lax.axis_index("wa"), lax.axis_index("ka") & 1]).astype(jnp.int32)

    operands = (place, weighted_values(place, coeff_val, miller), coeff_cond)
    opposite = [partial_momentum(k, (3,), *operands) for k in range(kcount)]
    neighbour = [partial_momentum(k, (2,), *operands) for k in range(kcount)]
    others = [partial_momentum(k, (1, 0), *operands) for k in range(kcount)]
    parts = [(own, second, first, both) for (both,), (first,), (second, own) in zip(opposite, neighbour, others)]
    chunks = [gathered_chunks(k, parts[k], pw_factor) for k in range(kcount)]
    operands = (place, weights, freqs, energy_val, energy_cond, orbit_val, orbit_cond)
    pair = []
    for k in range(kcount):
        own, second, first = chunks[k]
        pair = pair_sums(((k, (0,)),), *operands, {k: (own,)}, pair, 1)
        first, pair = lax.optimization_barrier((first, pair))
        half = first.shape[0] // 2
        passed = jnp.concatenate([cross(first[:half], k, 1), cross(second[half:], k, 0)])
        chunks[k] = (own, second, first, passed)
    pair = pair_sums(((0, (1, 2)), (1, (1, 2))), *operands, chunks, pair, 1)
    pair = pair_sums(((0, (3,)),), *operands, chunks, pair, 1)
    keep, send = pair_sums(((1, (3,)),), *operands, chunks, pair, 2)
    pair = keep + swap(send, "ka", 1)
    total = wing_sums(place, everyone(pair, "wa"), zeta)
    total = total + swap(total, "ka", 1)
    total = total + swap(total, "ka", 2)
    return pl.pallas_call(
        functools.partial(final_kernel, float(2 * ways)),
        out_shape=[
            jax.ShapeDtypeStruct((3, nfreq, slab_rows), F32),
            jax.ShapeDtypeStruct((3, nfreq), F32),
        ],
        in_specs=[VMEM] * 2,
        out_specs=[VMEM] * 2,
        compiler_params=pltpu.CompilerParams(vmem_limit_bytes=4 << 20),
        name="final",
    )(total, swap(total, "ka", 6))


def solution(mesh):
    return jax.shard_map(
        local,
        mesh=mesh,
        in_specs=(
            P("ka", None, "wa"),
            P("ka", None, "wa"),
            P(None, "wa"),
            P("ka", None),
            P("ka", None),
            P("ka", None, "wa"),
            P("ka", None, "wa"),
            P("wa", None),
            P(),
            P("ka"),
        ),
        out_specs=(P(None, None, "wa"), P()),
        check_vma=False,
    )
```

```python
import functools

import jax
import jax.numpy as jnp
from jax import lax
from jax.experimental import pallas as pl
from jax.experimental.pallas import tpu as pltpu
from jax.sharding import PartitionSpec as P

MASKS = (((8, 24, 1, 3, 4), (24, 8, 3, 1, 4)), ((1, 3, 8, 24, 4), (3, 1, 24, 8, 4)))
CB, VB = 4, 8
F32, BF16 = jnp.float32, jnp.bfloat16
VMEM, SMEM = pl.BlockSpec(memory_space=pltpu.VMEM), pl.BlockSpec(memory_space=pltpu.SMEM)

def code_of(place, kpoint):
    index, core = place[0], place[1]
    x, z, y = index >> 3, (index >> 2) & 1, index & 3


    def pairs(along):
        one, two = (along ^ (along >> 1)) & 1, along >> 1
        return (one << 1 | two) + ((two << 1 | one) - (one << 1 | two)) * core

    first, second = (x, y) if kpoint == 0 else (y, x)
    return pairs(first), pairs(second) << 1 | z


def swap(value, axis, mask):
    return lax.ppermute(value, axis, [(i, i ^ mask) for i in range(lax.axis_size(axis))])


def cross(value, kpoint, *dims):
    groups, ways = lax.axis_size("ka"), lax.axis_size("wa")
    pairs = []
    for group in range(groups):
        mask = 0
        for dim in dims:
            mask ^= MASKS[kpoint][group & 1][dim]
        pairs += [(group * ways + i, group * ways + (i ^ mask)) for i in range(ways)]
    return lax.ppermute(value, ("ka", "wa"), pairs)


def everyone(value, axis):
    parts = lax.axis_size(axis)
    return lax.all_to_all(jnp.broadcast_to(value[None], (parts,) + value.shape), axis, 0, 0)


def gathered_chunks(kpoint, partial, factor):
    own, second, first, both = partial
    second = second + cross(both, kpoint, 0)
    one, two = cross(first, kpoint, 0), cross(second, kpoint, 1)

    half = VB // 2
    held = (own[:half] + one[:half]) + two[:half]
    held = held + cross((own[half:] + one[half:]) + two[half:], kpoint, 2)
    half = half // 2
    held = held[:half] + cross(held[half:], kpoint, 3)
    held = (held + cross(held, kpoint, 4)[::-1]) * factor
    for dim in (3, 2):
        held = jnp.concatenate([held, cross(held, kpoint, dim)])
    first, second = cross(held, kpoint, 0), cross(held, kpoint, 1)
    return held, second, first


def momentum_kernel(kpoint, quarters, place_ref, val_ref, miller_ref, cond_ref, *refs):
    outs, weighted = refs[:-1], refs[-1]
    nval = val_ref.shape[1]
    rows, cols = outs[0].shape[2:]
    me_c, me_v = code_of(place_ref, kpoint)
    for place in range(VB):
        source = pl.multiple_of((place ^ me_v) * rows, rows)
        block = val_ref[kpoint, pl.ds(source, rows), :].astype(F32)
        for axis in range(3):
            factor = miller_ref[axis : axis + 1, :].astype(F32)
            weighted[axis * nval + place * rows : axis * nval + (place + 1) * rows, :] = (
                block * factor
            ).astype(BF16)
    for quarter, out in zip(quarters, outs):
        start = pl.multiple_of((quarter ^ me_c) * cols, cols)
        result = lax.dot_general(
            weighted[...],
            cond_ref[kpoint, pl.ds(start, cols), :],
            (((1,), (1,)), ((), ())),
            preferred_element_type=F32,
        )
        for eighth in range(VB):
            for axis in range(3):
                start = axis * nval + eighth * rows
                out[eighth, axis] = result[start : start + rows]


def partial_momentum(kpoint, quarters, place, coeff_val, miller, coeff_cond):
    _, nval, depth = coeff_val.shape
    ncond = coeff_cond.shape[1]
    count = len(quarters)
    return pl.pallas_call(
        functools.partial(momentum_kernel, kpoint, quarters),
        out_shape=[jax.ShapeDtypeStruct((VB, 3, nval // VB, ncond // CB), F32)] * count,
        in_specs=[SMEM, VMEM, VMEM, VMEM],
        out_specs=[VMEM] * count,
        scratch_shapes=[pltpu.VMEM((3 * nval, depth), BF16)],
        cost_estimate=pl.CostEstimate(
            flops=2 * 3 * nval * ncond * depth * count // CB,
            bytes_accessed=(2 * nval + 2 * ncond * count // CB) * depth + 12 * nval * ncond * count // CB,
            transcendentals=0,
        ),
        compiler_params=pltpu.CompilerParams(vmem_limit_bytes=24 << 20),
        name="partial_momentum",
    )(place, coeff_val, miller, coeff_cond)


def pair_kernel(groups, place_ref, weight_ref, freq_ref, energy_val, energy_cond, orbit_val, orbit_cond, *refs):
    _, nval, points = orbit_val.shape
    ncond = orbit_cond.shape[1]
    nfreq = freq_ref.shape[0]
    count = sum(len(quarters) for _, quarters in groups)
    chunks, refs = refs[:count], refs[count:]
    begins = groups[0] == (0, (0,))
    before, refs = (None, refs) if begins else (refs[0], refs[1:])
    outs, (total, amplitude, level, orbits, weight) = refs[:-5], refs[-5:]
    rows, cols = chunks[0].shape[2:]
    scale = float(nval * ncond) ** (-0.5)
    tops = 3 * nfreq
    for spot, (k, quarters) in enumerate(groups):
        mine, chunks = chunks[: len(quarters)], chunks[len(quarters) :]
        depth = len(quarters) * cols
        me_c, me_v = code_of(place_ref, k)
        level[spot] = jnp.transpose(jnp.broadcast_to(energy_val[k : k + 1, :], (nval, nval)))
        top = []
        for part, quarter in enumerate(quarters):
            start = pl.multiple_of((quarter ^ me_c) * cols, cols)
            top.append(energy_cond[k : k + 1, pl.ds(start, cols)])
            orbits[spot, part * cols : (part + 1) * cols, :] = orbit_cond[k, pl.ds(start, cols), :]

        def bottom_of(where, spot=spot):
            return jnp.concatenate([level[spot, where, :]] * (cols // nval), axis=1)

        def factors_of(gap):
            square = gap * gap
            return [4.0 / (square + freq_ref[w] * freq_ref[w]) for w in range(nfreq)]

        def eighth(place, carry, k=k, spot=spot, me_v=me_v, top=top, mine=mine, bottom_of=bottom_of):
            here = pl.ds(pl.multiple_of(place * rows, rows), rows)
            there = pl.ds(pl.multiple_of((place ^ me_v) * rows, rows), rows)
            weight[spot, here, :] = orbit_val[k, there, :].astype(F32) * (weight_ref[k] * scale)
            bottom = bottom_of(there)
            for part, chunk in enumerate(mine):
                factors = factors_of(top[part] - bottom)
                for axis in range(3):
                    momentum = chunk[place, axis]
                    for w in range(nfreq):
                        start = pl.multiple_of((axis * nfreq + w) * nval + place * rows, rows)
                        amplitude[spot, pl.ds(start, rows), part * cols : (part + 1) * cols] = (
                            momentum * factors[w]
                        ).astype(BF16)
            return carry

        lax.fori_loop(0, VB, eighth, 0, unroll=2)
        for axis in range(3):
            start = axis * nfreq * nval
            expanded = jnp.dot(
                amplitude[spot, start : start + nfreq * nval, :depth],
                orbits[spot, :depth, :],
                preferred_element_type=F32,
            )
            for w in range(nfreq):
                row = slice(axis * nfreq + w, axis * nfreq + w + 1)
                value = jnp.sum(expanded[w * nval : (w + 1) * nval] * weight[spot], axis=0, keepdims=True)
                if spot > 0:
                    value = value + total[row, :]
                elif not begins:
                    value = value + before[row, :]
                total[row, :] = value

        if quarters[0] == 0:
            bottom = bottom_of(pl.ds(pl.multiple_of(me_v * rows, rows), rows))
            gap = top[0] - bottom
            ratios = [factor / gap for factor in factors_of(gap)]
            for axis in range(3):
                square = mine[0][0, axis] * mine[0][0, axis]
                row = slice(tops + axis, tops + axis + 1)
                for w in range(nfreq):
                    value = jnp.sum(square * ratios[w], axis=0, keepdims=True)
                    value = (value[:, :nval] + value[:, nval:]) * (weight_ref[k] / float(nval * ncond))
                    lanes = slice(w * nval, (w + 1) * nval)
                    total[row, lanes] = value if begins else value + before[row, lanes]
            row = slice(tops + 3, tops + 4)
            value = jnp.full((1, points), weight_ref[k], F32)
            total[row, :] = value if begins else value + before[row, :]
    if groups[0][1][0] != 0:
        total[tops:, :] = before[tops:, :]
    if len(outs) == 2:
        keep, send = outs
        across = points // 2
        keep[...] = total[:, pl.ds(pl.multiple_of(place_ref[1] * across, across), across)]
        send[...] = total[:, pl.ds(pl.multiple_of((1 - place_ref[1]) * across, across), across)]
    else:
        outs[0][...] = total[...]


def pair_sums(groups, place, weights, freqs, energy_val, energy_cond, orbit_val, orbit_cond, chunks, before, parts):
    _, nval, points = orbit_val.shape
    ncond = orbit_cond.shape[1]
    nfreq = freqs.shape[0]
    height = 3 * nfreq + 4
    depth = ncond // CB * max(len(quarters) for _, quarters in groups)
    count = len(groups)
    operands = [energy_val, energy_cond, orbit_val, orbit_cond]
    operands += [chunks[k][quarter] for k, quarters in groups for quarter in quarters]
    operands += before
    return list(
        pl.pallas_call(
            functools.partial(pair_kernel, groups),
            out_shape=[jax.ShapeDtypeStruct((height, points // parts), F32)] * parts,
            in_specs=[SMEM] * 3 + [VMEM] * len(operands),
            out_specs=[VMEM] * parts,
            scratch_shapes=[
                pltpu.VMEM((height, points), F32),
                pltpu.VMEM((count, 3 * nfreq * nval, depth), BF16),
                pltpu.VMEM((count, nval, nval), F32),
                pltpu.VMEM((count, depth, points), BF16),
                pltpu.VMEM((count, nval, points), F32),
            ],
            cost_estimate=pl.CostEstimate(
                flops=count * 2 * 3 * nfreq * nval * depth * points,
                bytes_accessed=count * (12 * nval * depth + 4 * depth * points),
                transcendentals=0,
            ),
            compiler_params=pltpu.CompilerParams(vmem_limit_bytes=20 << 20),
            name="pair_sums",
        )(place, weights, freqs, *operands)
    )


def wing_kernel(place_ref, gathered, zeta, out):
    ways, height, points = gathered.shape
    slab_rows = zeta.shape[0]
    tops = height - 4
    total = jnp.zeros((3 * height, slab_rows), F32)
    last = jnp.zeros((4, points), F32)
    for device in range(ways):
        value = gathered[device]
        last = last + value[tops:]
        pieces = []
        for _ in range(3):
            rounded = value.astype(BF16)
            pieces.append(rounded)
            value = value - rounded.astype(F32)
        start = pl.multiple_of((2 * device + place_ref[1]) * points, points)
        total = total + lax.dot_general(
            jnp.concatenate(pieces, axis=0),
            zeta[:, pl.ds(start, points)],
            (((1,), (1,)), ((), ())),
            preferred_element_type=F32,
        )
    total = total[:height] + total[height : 2 * height] + total[2 * height :]
    out[:tops] = total[:tops]
    lane = lax.broadcasted_iota(jnp.int32, (3, slab_rows), 1)
    across = points // 2
    head = jnp.zeros((3, slab_rows), F32)
    for tile in range(2):
        value = jnp.sum(last[:3, tile * across : (tile + 1) * across], axis=1, keepdims=True)
        head = jnp.where(lane == 2 * place_ref[1] + tile, value, head)
    out[tops : tops + 3] = head
    out[tops + 3 :] = last[3:, :slab_rows]


def wing_sums(place, gathered, zeta):
    ways, height, points = gathered.shape
    slab_rows = zeta.shape[0]
    return pl.pallas_call(
        wing_kernel,
        out_shape=jax.ShapeDtypeStruct((height, slab_rows), F32),
        in_specs=[SMEM, VMEM, VMEM],
        out_specs=VMEM,
        cost_estimate=pl.CostEstimate(
            flops=6 * height * slab_rows * ways * points,
            bytes_accessed=4 * slab_rows * ways * points + 4 * height * ways * points,
            transcendentals=0,
        ),
        compiler_params=pltpu.CompilerParams(vmem_limit_bytes=20 << 20),
        name="wing_sums",
    )(place, gathered, zeta)


def final_kernel(copies, one, two, wing, head):
    total = one[...] + two[...]
    tops = total.shape[0] - 4
    nfreq = wing.shape[1]
    scale = copies / total[tops + 3 :]
    for axis in range(3):
        wing[axis] = total[axis * nfreq : (axis + 1) * nfreq] * scale
    head[...] = total[tops : tops + 3, :nfreq] * scale[:, :nfreq]


def local(
    coeff_val,
    coeff_cond,
    miller,
    energy_val,
    energy_cond,
    orbit_val,
    orbit_cond,
    zeta,
    freqs,
    kweight,
):
    kcount, nval, npw_dev = coeff_val.shape
    nfreq = freqs.shape[0]
    slab_rows = zeta.shape[0]
    ways = lax.axis_size("wa")
    pw_factor = float(npw_dev * ways) ** (-0.5)
    weights = kweight.astype(F32)
    place = jnp.stack([lax.axis_index("wa"), lax.axis_index("ka") & 1]).astype(jnp.int32)

    operands = (place, coeff_val, miller, coeff_cond)
    sends = [partial_momentum(k, (3, 2), *operands) for k in range(kcount)]
    keeps = [partial_momentum(k, (1, 0), *operands) for k in range(kcount)]
    parts = [(own, second, first, both) for (both, first), (second, own) in zip(sends, keeps)]
    chunks = [gathered_chunks(k, parts[k], pw_factor) for k in range(kcount)]
    operands = (place, weights, freqs, energy_val, energy_cond, orbit_val, orbit_cond)
    pair = []
    for k in range(kcount):
        own, second, first = chunks[k]
        pair = pair_sums(((k, (0,)),), *operands, {k: (own,)}, pair, 1)
        first, pair = lax.optimization_barrier((first, pair))
        chunks[k] = (own, second, first, cross(first, k, 1))
    pair = pair_sums(((0, (1, 2)), (1, (1, 2))), *operands, chunks, pair, 1)
    pair = pair_sums(((0, (3,)),), *operands, chunks, pair, 1)
    keep, send = pair_sums(((1, (3,)),), *operands, chunks, pair, 2)
    pair = keep + swap(send, "ka", 1)
    total = wing_sums(place, everyone(pair, "wa"), zeta)
    total = total + swap(total, "ka", 1)
    total = total + swap(total, "ka", 2)
    return pl.pallas_call(
        functools.partial(final_kernel, float(2 * ways)),
        out_shape=[
            jax.ShapeDtypeStruct((3, nfreq, slab_rows), F32),
            jax.ShapeDtypeStruct((3, nfreq), F32),
        ],
        in_specs=[VMEM] * 2,
        out_specs=[VMEM] * 2,
        compiler_params=pltpu.CompilerParams(vmem_limit_bytes=4 << 20),
        name="final",
    )(total, swap(total, "ka", 6))


def solution(mesh):
    return jax.shard_map(
        local,
        mesh=mesh,
        in_specs=(
            P("ka", None, "wa"),
            P("ka", None, "wa"),
            P(None, "wa"),
            P("ka", None),
            P("ka", None),
            P("ka", None, "wa"),
            P("ka", None, "wa"),
            P("wa", None),
            P(),
            P("ka"),
        ),
        out_specs=(P(None, None, "wa"), P()),
        check_vma=False,
    )
```

```python
import functools

import jax
import jax.numpy as jnp
from jax import lax
from jax.experimental import pallas as pl
from jax.experimental.pallas import tpu as pltpu
from jax.sharding import PartitionSpec as P

MASKS = (((8, 24, 1, 3, 4), (24, 8, 1, 3, 4)), ((1, 3, 8, 24, 4), (3, 1, 8, 24, 4)))
CB, VB = 4, 8
F32, BF16 = jnp.float32, jnp.bfloat16
VMEM, SMEM = pl.BlockSpec(memory_space=pltpu.VMEM), pl.BlockSpec(memory_space=pltpu.SMEM)

def code_of(place, kpoint):
    index, core = place[0], place[1]
    x, z, y = index >> 3, (index >> 2) & 1, index & 3

    first, second = (x, y) if kpoint == 0 else (y, x)
    one, two = (first ^ (first >> 1)) & 1, first >> 1
    quarter = (one << 1 | two) + ((two << 1 | one) - (one << 1 | two)) * core
    return quarter, ((second ^ (second >> 1)) & 1) << 2 | (second >> 1) << 1 | z


def swap(value, axis, mask):
    return lax.ppermute(value, axis, [(i, i ^ mask) for i in range(lax.axis_size(axis))])


def cross(value, kpoint, *dims):
    groups, ways = lax.axis_size("ka"), lax.axis_size("wa")
    pairs = []
    for group in range(groups):
        mask = 0
        for dim in dims:
            mask ^= MASKS[kpoint][group & 1][dim]
        pairs += [(group * ways + i, group * ways + (i ^ mask)) for i in range(ways)]
    return lax.ppermute(value, ("ka", "wa"), pairs)


def around(value, kpoint, dim):
    return swap(value, "wa", MASKS[kpoint][0][dim])


def everyone(value, axis):
    parts = lax.axis_size(axis)
    return lax.all_to_all(jnp.broadcast_to(value[None], (parts,) + value.shape), axis, 0, 0)


def gathered_chunks(kpoint, partial, factor):
    own, second, first, both = partial
    second = second + cross(both, kpoint, 0)
    one, two = cross(first, kpoint, 0), cross(second, kpoint, 1)

    def summed(place):
        lines = slice(2 * place, 2 * place + 2)
        return (own[lines] + one[lines]) + two[lines]

    held = (summed(0) + cross(summed(2), kpoint, 2)) + (
        cross(summed(1), kpoint, 3) + cross(summed(3), kpoint, 2, 3)
    )
    held = (held + cross(held, kpoint, 4)[::-1]) * factor
    others = [cross(held, kpoint, *dims) for dims in ((3,), (2,), (2, 3))]
    held = jnp.concatenate([held] + others)
    return held, around(held, kpoint, 1), around(held, kpoint, 0)


def momentum_kernel(kpoint, quarters, place_ref, val_ref, miller_ref, cond_ref, *refs):
    outs, weighted = refs[:-1], refs[-1]
    nval = val_ref.shape[1]
    rows, cols = outs[0].shape[2:]
    me_c, me_v = code_of(place_ref, kpoint)
    for place in range(VB):
        source = pl.multiple_of((place ^ me_v) * rows, rows)
        block = val_ref[kpoint, pl.ds(source, rows), :].astype(F32)
        for axis in range(3):
            factor = miller_ref[axis : axis + 1, :].astype(F32)
            weighted[axis * nval + place * rows : axis * nval + (place + 1) * rows, :] = (
                block * factor
            ).astype(BF16)
    for quarter, out in zip(quarters, outs):
        start = pl.multiple_of((quarter ^ me_c) * cols, cols)
        result = lax.dot_general(
            weighted[...],
            cond_ref[kpoint, pl.ds(start, cols), :],
            (((1,), (1,)), ((), ())),
            preferred_element_type=F32,
        )
        for eighth in range(VB):
            for axis in range(3):
                start = axis * nval + eighth * rows
                out[eighth, axis] = result[start : start + rows]


def partial_momentum(kpoint, quarters, place, coeff_val, miller, coeff_cond):
    _, nval, depth = coeff_val.shape
    ncond = coeff_cond.shape[1]
    count = len(quarters)
    return pl.pallas_call(
        functools.partial(momentum_kernel, kpoint, quarters),
        out_shape=[jax.ShapeDtypeStruct((VB, 3, nval // VB, ncond // CB), F32)] * count,
        in_specs=[SMEM, VMEM, VMEM, VMEM],
        out_specs=[VMEM] * count,
        scratch_shapes=[pltpu.VMEM((3 * nval, depth), BF16)],
        cost_estimate=pl.CostEstimate(
            flops=2 * 3 * nval * ncond * depth * count // CB,
            bytes_accessed=(2 * nval + 2 * ncond * count // CB) * depth + 12 * nval * ncond * count // CB,
            transcendentals=0,
        ),
        compiler_params=pltpu.CompilerParams(vmem_limit_bytes=24 << 20),
        name="partial_momentum",
    )(place, coeff_val, miller, coeff_cond)


def pair_kernel(groups, place_ref, weight_ref, freq_ref, energy_val, energy_cond, orbit_val, orbit_cond, *refs):
    _, nval, points = orbit_val.shape
    ncond = orbit_cond.shape[1]
    nfreq = freq_ref.shape[0]
    count = sum(len(quarters) for _, quarters in groups)
    chunks, refs = refs[:count], refs[count:]
    begins = groups[0][1][0] == 0
    before, refs = (None, refs) if begins else (refs[0], refs[1:])
    outs, (total, amplitude, level, orbits, weight) = refs[:-5], refs[-5:]
    rows, cols = chunks[0].shape[2:]
    scale = float(nval * ncond) ** (-0.5)
    tops = 3 * nfreq
    for spot, (k, quarters) in enumerate(groups):
        mine, chunks = chunks[: len(quarters)], chunks[len(quarters) :]
        depth = len(quarters) * cols
        me_c, me_v = code_of(place_ref, k)
        level[spot] = jnp.transpose(jnp.broadcast_to(energy_val[k : k + 1, :], (nval, nval)))
        top = []
        for part, quarter in enumerate(quarters):
            if quarter in (1, 2):
                quarter = quarter + (3 - 2 * quarter) * place_ref[1]
            start = pl.multiple_of((quarter ^ me_c) * cols, cols)
            top.append(energy_cond[k : k + 1, pl.ds(start, cols)])
            orbits[spot, part * cols : (part + 1) * cols, :] = orbit_cond[k, pl.ds(start, cols), :]

        def bottom_of(where, spot=spot):
            return jnp.concatenate([level[spot, where, :]] * (cols // nval), axis=1)

        def factors_of(gap):
            square = gap * gap
            return [4.0 / (square + freq_ref[w] * freq_ref[w]) for w in range(nfreq)]

        def eighth(place, carry, k=k, spot=spot, me_v=me_v, top=top, mine=mine, bottom_of=bottom_of):
            here = pl.ds(pl.multiple_of(place * rows, rows), rows)
            there = pl.ds(pl.multiple_of((place ^ me_v) * rows, rows), rows)
            weight[spot, here, :] = orbit_val[k, there, :].astype(F32) * (weight_ref[k] * scale)
            bottom = bottom_of(there)
            for part, chunk in enumerate(mine):
                factors = factors_of(top[part] - bottom)
                for axis in range(3):
                    momentum = chunk[place, axis]
                    for w in range(nfreq):
                        start = pl.multiple_of((axis * nfreq + w) * nval + place * rows, rows)
                        amplitude[spot, pl.ds(start, rows), part * cols : (part + 1) * cols] = (
                            momentum * factors[w]
                        ).astype(BF16)
            return carry

        lax.fori_loop(0, VB, eighth, 0, unroll=2)
        for axis in range(3):
            start = axis * nfreq * nval
            expanded = jnp.dot(
                amplitude[spot, start : start + nfreq * nval, :depth],
                orbits[spot, :depth, :],
                preferred_element_type=F32,
            )
            for w in range(nfreq):
                row = slice(axis * nfreq + w, axis * nfreq + w + 1)
                value = jnp.sum(expanded[w * nval : (w + 1) * nval] * weight[spot], axis=0, keepdims=True)
                if spot > 0:
                    value = value + total[row, :]
                elif not begins:
                    value = value + before[row, :]
                total[row, :] = value

        if begins:
            bottom = bottom_of(pl.ds(pl.multiple_of(me_v * rows, rows), rows))
            gap = top[0] - bottom
            ratios = [factor / gap for factor in factors_of(gap)]
            for axis in range(3):
                square = mine[0][0, axis] * mine[0][0, axis]
                row = slice(tops + axis, tops + axis + 1)
                for w in range(nfreq):
                    value = jnp.sum(square * ratios[w], axis=0, keepdims=True)
                    value = (value[:, :nval] + value[:, nval:]) * (weight_ref[k] / float(nval * ncond))
                    lanes = slice(w * nval, (w + 1) * nval)
                    total[row, lanes] = value + total[row, lanes] if spot else value
            row = slice(tops + 3, tops + 4)
            value = jnp.full((1, points), weight_ref[k], F32)
            total[row, :] = value + total[row, :] if spot else value
    if not begins:
        total[tops:, :] = before[tops:, :]
    if len(outs) == 2:
        keep, send = outs
        across = points // 2
        keep[...] = total[:, pl.ds(pl.multiple_of(place_ref[1] * across, across), across)]
        send[...] = total[:, pl.ds(pl.multiple_of((1 - place_ref[1]) * across, across), across)]
    else:
        outs[0][...] = total[...]


def pair_sums(groups, place, weights, freqs, energy_val, energy_cond, orbit_val, orbit_cond, chunks, before, parts):
    _, nval, points = orbit_val.shape
    ncond = orbit_cond.shape[1]
    nfreq = freqs.shape[0]
    height = 3 * nfreq + 4
    depth = ncond // CB * max(len(quarters) for _, quarters in groups)
    count = len(groups)
    operands = [energy_val, energy_cond, orbit_val, orbit_cond]
    operands += [chunks[k][quarter] for k, quarters in groups for quarter in quarters]
    operands += before
    return list(
        pl.pallas_call(
            functools.partial(pair_kernel, groups),
            out_shape=[jax.ShapeDtypeStruct((height, points // parts), F32)] * parts,
            in_specs=[SMEM] * 3 + [VMEM] * len(operands),
            out_specs=[VMEM] * parts,
            scratch_shapes=[
                pltpu.VMEM((height, points), F32),
                pltpu.VMEM((count, 3 * nfreq * nval, depth), BF16),
                pltpu.VMEM((count, nval, nval), F32),
                pltpu.VMEM((count, depth, points), BF16),
                pltpu.VMEM((count, nval, points), F32),
            ],
            cost_estimate=pl.CostEstimate(
                flops=count * 2 * 3 * nfreq * nval * depth * points,
                bytes_accessed=count * (12 * nval * depth + 4 * depth * points),
                transcendentals=0,
            ),
            compiler_params=pltpu.CompilerParams(vmem_limit_bytes=20 << 20),
            name="pair_sums",
        )(place, weights, freqs, *operands)
    )


def wing_kernel(place_ref, gathered, zeta, out):
    ways, height, points = gathered.shape
    slab_rows = zeta.shape[0]
    tops = height - 4
    total = jnp.zeros((3 * height, slab_rows), F32)
    last = jnp.zeros((4, points), F32)
    for device in range(ways):
        value = gathered[device]
        last = last + value[tops:]
        pieces = []
        for _ in range(3):
            rounded = value.astype(BF16)
            pieces.append(rounded)
            value = value - rounded.astype(F32)
        start = pl.multiple_of((2 * device + place_ref[1]) * points, points)
        total = total + lax.dot_general(
            jnp.concatenate(pieces, axis=0),
            zeta[:, pl.ds(start, points)],
            (((1,), (1,)), ((), ())),
            preferred_element_type=F32,
        )
    total = total[:height] + total[height : 2 * height] + total[2 * height :]
    out[:tops] = total[:tops]
    lane = lax.broadcasted_iota(jnp.int32, (3, slab_rows), 1)
    across = points // 2
    head = jnp.zeros((3, slab_rows), F32)
    for tile in range(2):
        value = jnp.sum(last[:3, tile * across : (tile + 1) * across], axis=1, keepdims=True)
        head = jnp.where(lane == 2 * place_ref[1] + tile, value, head)
    out[tops : tops + 3] = head
    out[tops + 3 :] = last[3:, :slab_rows]


def wing_sums(place, gathered, zeta):
    ways, height, points = gathered.shape
    slab_rows = zeta.shape[0]
    return pl.pallas_call(
        wing_kernel,
        out_shape=jax.ShapeDtypeStruct((height, slab_rows), F32),
        in_specs=[SMEM, VMEM, VMEM],
        out_specs=VMEM,
        cost_estimate=pl.CostEstimate(
            flops=6 * height * slab_rows * ways * points,
            bytes_accessed=4 * slab_rows * ways * points + 4 * height * ways * points,
            transcendentals=0,
        ),
        compiler_params=pltpu.CompilerParams(vmem_limit_bytes=20 << 20),
        name="wing_sums",
    )(place, gathered, zeta)


def final_kernel(copies, one, two, wing, head):
    total = one[...] + two[...]
    tops = total.shape[0] - 4
    nfreq = wing.shape[1]
    scale = copies / total[tops + 3 :]
    for axis in range(3):
        wing[axis] = total[axis * nfreq : (axis + 1) * nfreq] * scale
    head[...] = total[tops : tops + 3, :nfreq] * scale[:, :nfreq]


def local(
    coeff_val,
    coeff_cond,
    miller,
    energy_val,
    energy_cond,
    orbit_val,
    orbit_cond,
    zeta,
    freqs,
    kweight,
):
    kcount, nval, npw_dev = coeff_val.shape
    nfreq = freqs.shape[0]
    slab_rows = zeta.shape[0]
    ways = lax.axis_size("wa")
    pw_factor = float(npw_dev * ways) ** (-0.5)
    weights = kweight.astype(F32)
    place = jnp.stack([lax.axis_index("wa"), lax.axis_index("ka") & 1]).astype(jnp.int32)

    operands = (place, coeff_val, miller, coeff_cond)
    sends = [partial_momentum(k, (3, 2), *operands) for k in range(kcount)]
    keeps = [partial_momentum(k, (1, 0), *operands) for k in range(kcount)]
    parts = [(own, second, first, both) for (both, first), (second, own) in zip(sends, keeps)]
    chunks = [gathered_chunks(k, parts[k], pw_factor) for k in range(kcount)]
    operands = (place, weights, freqs, energy_val, energy_cond, orbit_val, orbit_cond)
    own, second, first = chunks[0]
    chunks[0] = (own, second, first, around(first, 0, 1))
    own, second, first = chunks[1]
    pair = pair_sums(((0, (0,)), (1, (0,))), *operands, chunks, [], 1)
    first, pair = lax.optimization_barrier((first, pair))
    chunks[1] = (own, second, first, around(first, 1, 1))
    for k in range(kcount):
        pair = pair_sums(((k, (1, 2)),), *operands, chunks, pair, 1)
    pair = pair_sums(((0, (3,)),), *operands, chunks, pair, 1)
    keep, send = pair_sums(((1, (3,)),), *operands, chunks, pair, 2)
    pair = keep + swap(send, "ka", 1)
    total = wing_sums(place, everyone(pair, "wa"), zeta)
    total = total + swap(total, "ka", 1)
    total = total + swap(total, "ka", 2)
    return pl.pallas_call(
        functools.partial(final_kernel, float(2 * ways)),
        out_shape=[
            jax.ShapeDtypeStruct((3, nfreq, slab_rows), F32),
            jax.ShapeDtypeStruct((3, nfreq), F32),
        ],
        in_specs=[VMEM] * 2,
        out_specs=[VMEM] * 2,
        compiler_params=pltpu.CompilerParams(vmem_limit_bytes=4 << 20),
        name="final",
    )(total, swap(total, "ka", 6))


def solution(mesh):
    return jax.shard_map(
        local,
        mesh=mesh,
        in_specs=(
            P("ka", None, "wa"),
            P("ka", None, "wa"),
            P(None, "wa"),
            P("ka", None),
            P("ka", None),
            P("ka", None, "wa"),
            P("ka", None, "wa"),
            P("wa", None),
            P(),
            P("ka"),
        ),
        out_specs=(P(None, None, "wa"), P()),
        check_vma=False,
    )
```

```python
import functools

import jax
import jax.numpy as jnp
from jax import lax
from jax.experimental import pallas as pl
from jax.experimental.pallas import tpu as pltpu
from jax.sharding import PartitionSpec as P

MASKS = (((8, 24, 1, 3, 4), (24, 8, 1, 3, 4)), ((1, 3, 8, 24, 4), (3, 1, 8, 24, 4)))
CB, VB = 4, 8
F32, BF16 = jnp.float32, jnp.bfloat16
VMEM, SMEM = pl.BlockSpec(memory_space=pltpu.VMEM), pl.BlockSpec(memory_space=pltpu.SMEM)

def code_of(place, kpoint):
    index, core = place[0], place[1]
    x, z, y = index >> 3, (index >> 2) & 1, index & 3

    first, second = (x, y) if kpoint == 0 else (y, x)
    one, two = (first ^ (first >> 1)) & 1, first >> 1
    quarter = (one << 1 | two) + ((two << 1 | one) - (one << 1 | two)) * core
    return quarter, ((second ^ (second >> 1)) & 1) << 2 | (second >> 1) << 1 | z


def swap(value, axis, mask):
    return lax.ppermute(value, axis, [(i, i ^ mask) for i in range(lax.axis_size(axis))])


def cross(value, kpoint, *dims):
    groups, ways = lax.axis_size("ka"), lax.axis_size("wa")
    pairs = []
    for group in range(groups):
        mask = 0
        for dim in dims:
            mask ^= MASKS[kpoint][group & 1][dim]
        pairs += [(group * ways + i, group * ways + (i ^ mask)) for i in range(ways)]
    return lax.ppermute(value, ("ka", "wa"), pairs)


def around(value, kpoint, dim):
    return swap(value, "wa", MASKS[kpoint][0][dim])


def everyone(value, axis):
    parts = lax.axis_size(axis)
    return lax.all_to_all(jnp.broadcast_to(value[None], (parts,) + value.shape), axis, 0, 0)


def gathered_chunks(kpoint, partial, factor):
    own, second, first, both = partial
    second = second + cross(both, kpoint, 0)
    one, two = cross(first, kpoint, 0), cross(second, kpoint, 1)

    def summed(place):
        lines = slice(2 * place, 2 * place + 2)
        return (own[lines] + one[lines]) + two[lines]

    held = (summed(0) + cross(summed(2), kpoint, 2)) + (
        cross(summed(1), kpoint, 3) + cross(summed(3), kpoint, 2, 3)
    )
    held = (held + cross(held, kpoint, 4)[::-1]) * factor
    others = [cross(held, kpoint, *dims) for dims in ((3,), (2,), (2, 3))]
    held = jnp.concatenate([held] + others)
    return held, around(held, kpoint, 1), around(held, kpoint, 0)


def momentum_kernel(kpoint, quarters, place_ref, val_ref, miller_ref, cond_ref, *refs):
    outs, weighted = refs[:-1], refs[-1]
    nval = val_ref.shape[1]
    rows, cols = outs[0].shape[2:]
    me_c, me_v = code_of(place_ref, kpoint)
    for place in range(VB):
        source = pl.multiple_of((place ^ me_v) * rows, rows)
        block = val_ref[kpoint, pl.ds(source, rows), :].astype(F32)
        for axis in range(3):
            factor = miller_ref[axis : axis + 1, :].astype(F32)
            weighted[axis * nval + place * rows : axis * nval + (place + 1) * rows, :] = (
                block * factor
            ).astype(BF16)
    for quarter, out in zip(quarters, outs):
        start = pl.multiple_of((quarter ^ me_c) * cols, cols)
        result = lax.dot_general(
            weighted[...],
            cond_ref[kpoint, pl.ds(start, cols), :],
            (((1,), (1,)), ((), ())),
            preferred_element_type=F32,
        )
        for eighth in range(VB):
            for axis in range(3):
                start = axis * nval + eighth * rows
                out[eighth, axis] = result[start : start + rows]


def partial_momentum(kpoint, quarters, place, coeff_val, miller, coeff_cond):
    _, nval, depth = coeff_val.shape
    ncond = coeff_cond.shape[1]
    count = len(quarters)
    return pl.pallas_call(
        functools.partial(momentum_kernel, kpoint, quarters),
        out_shape=[jax.ShapeDtypeStruct((VB, 3, nval // VB, ncond // CB), F32)] * count,
        in_specs=[SMEM, VMEM, VMEM, VMEM],
        out_specs=[VMEM] * count,
        scratch_shapes=[pltpu.VMEM((3 * nval, depth), BF16)],
        cost_estimate=pl.CostEstimate(
            flops=2 * 3 * nval * ncond * depth * count // CB,
            bytes_accessed=(2 * nval + 2 * ncond * count // CB) * depth + 12 * nval * ncond * count // CB,
            transcendentals=0,
        ),
        compiler_params=pltpu.CompilerParams(vmem_limit_bytes=24 << 20),
        name="partial_momentum",
    )(place, coeff_val, miller, coeff_cond)


def pair_kernel(groups, place_ref, weight_ref, freq_ref, energy_val, energy_cond, orbit_val, orbit_cond, *refs):
    _, nval, points = orbit_val.shape
    ncond = orbit_cond.shape[1]
    nfreq = freq_ref.shape[0]
    count = sum(len(quarters) for _, quarters in groups)
    chunks, refs = refs[:count], refs[count:]
    begins = groups[0][1][0] == 0
    before, refs = (None, refs) if begins else (refs[0], refs[1:])
    outs, (total, amplitude, level, orbits, weight) = refs[:-5], refs[-5:]
    rows, cols = chunks[0].shape[2:]
    scale = float(nval * ncond) ** (-0.5)
    tops = 3 * nfreq
    for spot, (k, quarters) in enumerate(groups):
        mine, chunks = chunks[: len(quarters)], chunks[len(quarters) :]
        depth = len(quarters) * cols
        me_c, me_v = code_of(place_ref, k)
        level[spot] = jnp.transpose(jnp.broadcast_to(energy_val[k : k + 1, :], (nval, nval)))
        top = []
        for part, quarter in enumerate(quarters):
            if quarter in (1, 2):
                quarter = quarter + (3 - 2 * quarter) * place_ref[1]
            start = pl.multiple_of((quarter ^ me_c) * cols, cols)
            top.append(energy_cond[k : k + 1, pl.ds(start, cols)])
            orbits[spot, part * cols : (part + 1) * cols, :] = orbit_cond[k, pl.ds(start, cols), :]

        def bottom_of(where, spot=spot):
            return jnp.concatenate([level[spot, where, :]] * (cols // nval), axis=1)

        def factors_of(gap):
            square = gap * gap
            return [4.0 / (square + freq_ref[w] * freq_ref[w]) for w in range(nfreq)]

        def eighth(place, carry, k=k, spot=spot, me_v=me_v, top=top, mine=mine, bottom_of=bottom_of):
            here = pl.ds(pl.multiple_of(place * rows, rows), rows)
            there = pl.ds(pl.multiple_of((place ^ me_v) * rows, rows), rows)
            weight[spot, here, :] = orbit_val[k, there, :].astype(F32) * (weight_ref[k] * scale)
            bottom = bottom_of(there)
            for part, chunk in enumerate(mine):
                factors = factors_of(top[part] - bottom)
                for axis in range(3):
                    momentum = chunk[place, axis]
                    for w in range(nfreq):
                        start = pl.multiple_of((axis * nfreq + w) * nval + place * rows, rows)
                        amplitude[spot, pl.ds(start, rows), part * cols : (part + 1) * cols] = (
                            momentum * factors[w]
                        ).astype(BF16)
            return carry

        lax.fori_loop(0, VB, eighth, 0, unroll=2)
        for axis in range(3):
            start = axis * nfreq * nval
            expanded = jnp.dot(
                amplitude[spot, start : start + nfreq * nval, :depth],
                orbits[spot, :depth, :],
                preferred_element_type=F32,
            )
            for w in range(nfreq):
                row = slice(axis * nfreq + w, axis * nfreq + w + 1)
                value = jnp.sum(expanded[w * nval : (w + 1) * nval] * weight[spot], axis=0, keepdims=True)
                if spot > 0:
                    value = value + total[row, :]
                elif not begins:
                    value = value + before[row, :]
                total[row, :] = value

        if begins:
            bottom = bottom_of(pl.ds(pl.multiple_of(me_v * rows, rows), rows))
            gap = top[0] - bottom
            ratios = [factor / gap for factor in factors_of(gap)]
            for axis in range(3):
                square = mine[0][0, axis] * mine[0][0, axis]
                row = slice(tops + axis, tops + axis + 1)
                for w in range(nfreq):
                    value = jnp.sum(square * ratios[w], axis=0, keepdims=True)
                    value = (value[:, :nval] + value[:, nval:]) * (weight_ref[k] / float(nval * ncond))
                    lanes = slice(w * nval, (w + 1) * nval)
                    total[row, lanes] = value + total[row, lanes] if spot else value
            row = slice(tops + 3, tops + 4)
            value = jnp.full((1, points), weight_ref[k], F32)
            total[row, :] = value + total[row, :] if spot else value
    if not begins:
        total[tops:, :] = before[tops:, :]
    if len(outs) == 2:
        keep, send = outs
        across = points // 2
        keep[...] = total[:, pl.ds(pl.multiple_of(place_ref[1] * across, across), across)]
        send[...] = total[:, pl.ds(pl.multiple_of((1 - place_ref[1]) * across, across), across)]
    else:
        outs[0][...] = total[...]


def pair_sums(groups, place, weights, freqs, energy_val, energy_cond, orbit_val, orbit_cond, chunks, before, parts):
    _, nval, points = orbit_val.shape
    ncond = orbit_cond.shape[1]
    nfreq = freqs.shape[0]
    height = 3 * nfreq + 4
    depth = ncond // CB * max(len(quarters) for _, quarters in groups)
    count = len(groups)
    operands = [energy_val, energy_cond, orbit_val, orbit_cond]
    operands += [chunks[k][quarter] for k, quarters in groups for quarter in quarters]
    operands += before
    return list(
        pl.pallas_call(
            functools.partial(pair_kernel, groups),
            out_shape=[jax.ShapeDtypeStruct((height, points // parts), F32)] * parts,
            in_specs=[SMEM] * 3 + [VMEM] * len(operands),
            out_specs=[VMEM] * parts,
            scratch_shapes=[
                pltpu.VMEM((height, points), F32),
                pltpu.VMEM((count, 3 * nfreq * nval, depth), BF16),
                pltpu.VMEM((count, nval, nval), F32),
                pltpu.VMEM((count, depth, points), BF16),
                pltpu.VMEM((count, nval, points), F32),
            ],
            cost_estimate=pl.CostEstimate(
                flops=count * 2 * 3 * nfreq * nval * depth * points,
                bytes_accessed=count * (12 * nval * depth + 4 * depth * points),
                transcendentals=0,
            ),
            compiler_params=pltpu.CompilerParams(vmem_limit_bytes=20 << 20),
            name="pair_sums",
        )(place, weights, freqs, *operands)
    )


def wing_kernel(place_ref, gathered, zeta, out):
    ways, height, points = gathered.shape
    slab_rows = zeta.shape[0]
    tops = height - 4
    total = jnp.zeros((3 * height, slab_rows), F32)
    last = jnp.zeros((4, points), F32)
    for device in range(ways):
        value = gathered[device]
        last = last + value[tops:]
        pieces = []
        for _ in range(3):
            rounded = value.astype(BF16)
            pieces.append(rounded)
            value = value - rounded.astype(F32)
        start = pl.multiple_of((2 * device + place_ref[1]) * points, points)
        total = total + lax.dot_general(
            jnp.concatenate(pieces, axis=0),
            zeta[:, pl.ds(start, points)],
            (((1,), (1,)), ((), ())),
            preferred_element_type=F32,
        )
    total = total[:height] + total[height : 2 * height] + total[2 * height :]
    out[:tops] = total[:tops]
    lane = lax.broadcasted_iota(jnp.int32, (3, slab_rows), 1)
    across = points // 2
    head = jnp.zeros((3, slab_rows), F32)
    for tile in range(2):
        value = jnp.sum(last[:3, tile * across : (tile + 1) * across], axis=1, keepdims=True)
        head = jnp.where(lane == 2 * place_ref[1] + tile, value, head)
    out[tops : tops + 3] = head
    out[tops + 3 :] = last[3:, :slab_rows]


def wing_sums(place, gathered, zeta):
    ways, height, points = gathered.shape
    slab_rows = zeta.shape[0]
    return pl.pallas_call(
        wing_kernel,
        out_shape=jax.ShapeDtypeStruct((height, slab_rows), F32),
        in_specs=[SMEM, VMEM, VMEM],
        out_specs=VMEM,
        cost_estimate=pl.CostEstimate(
            flops=6 * height * slab_rows * ways * points,
            bytes_accessed=4 * slab_rows * ways * points + 4 * height * ways * points,
            transcendentals=0,
        ),
        compiler_params=pltpu.CompilerParams(vmem_limit_bytes=20 << 20),
        name="wing_sums",
    )(place, gathered, zeta)


def final_kernel(copies, one, two, wing, head):
    total = one[...] + two[...]
    tops = total.shape[0] - 4
    nfreq = wing.shape[1]
    scale = copies / total[tops + 3 :]
    for axis in range(3):
        wing[axis] = total[axis * nfreq : (axis + 1) * nfreq] * scale
    head[...] = total[tops : tops + 3, :nfreq] * scale[:, :nfreq]


def local(
    coeff_val,
    coeff_cond,
    miller,
    energy_val,
    energy_cond,
    orbit_val,
    orbit_cond,
    zeta,
    freqs,
    kweight,
):
    kcount, nval, npw_dev = coeff_val.shape
    nfreq = freqs.shape[0]
    slab_rows = zeta.shape[0]
    ways = lax.axis_size("wa")
    pw_factor = float(npw_dev * ways) ** (-0.5)
    weights = kweight.astype(F32)
    place = jnp.stack([lax.axis_index("wa"), lax.axis_index("ka") & 1]).astype(jnp.int32)

    operands = (place, coeff_val, miller, coeff_cond)
    sends = [partial_momentum(k, (3, 2), *operands) for k in range(kcount)]
    keeps = [partial_momentum(k, (1, 0), *operands) for k in range(kcount)]
    parts = [(own, second, first, both) for (both, first), (second, own) in zip(sends, keeps)]
    chunks = [gathered_chunks(k, parts[k], pw_factor) for k in range(kcount)]
    operands = (place, weights, freqs, energy_val, energy_cond, orbit_val, orbit_cond)
    pair = pair_sums(((0, (0,)), (1, (0,))), *operands, chunks, [], 1)
    for k in range(kcount):
        own, second, first = chunks[k]
        if k == 0:
            first, pair = lax.optimization_barrier((first, pair))
        half = first.shape[0] // 2
        passed = jnp.concatenate([around(first[:half], k, 1), around(second[half:], k, 0)])
        chunks[k] = (own, second, first, passed)
    for k in range(kcount):
        pair = pair_sums(((k, (1, 2)),), *operands, chunks, pair, 1)
    pair = pair_sums(((0, (3,)),), *operands, chunks, pair, 1)
    keep, send = pair_sums(((1, (3,)),), *operands, chunks, pair, 2)
    pair = keep + swap(send, "ka", 1)
    total = wing_sums(place, everyone(pair, "wa"), zeta)
    total = total + swap(total, "ka", 1)
    total = total + swap(total, "ka", 2)
    return pl.pallas_call(
        functools.partial(final_kernel, float(2 * ways)),
        out_shape=[
            jax.ShapeDtypeStruct((3, nfreq, slab_rows), F32),
            jax.ShapeDtypeStruct((3, nfreq), F32),
        ],
        in_specs=[VMEM] * 2,
        out_specs=[VMEM] * 2,
        compiler_params=pltpu.CompilerParams(vmem_limit_bytes=4 << 20),
        name="final",
    )(total, swap(total, "ka", 6))


def solution(mesh):
    return jax.shard_map(
        local,
        mesh=mesh,
        in_specs=(
            P("ka", None, "wa"),
            P("ka", None, "wa"),
            P(None, "wa"),
            P("ka", None),
            P("ka", None),
            P("ka", None, "wa"),
            P("ka", None, "wa"),
            P("wa", None),
            P(),
            P("ka"),
        ),
        out_specs=(P(None, None, "wa"), P()),
        check_vma=False,
    )
```

```python
import functools

import jax
import jax.numpy as jnp
from jax import lax
from jax.experimental import pallas as pl
from jax.experimental.pallas import tpu as pltpu
from jax.sharding import PartitionSpec as P

MASKS = (((8, 24, 1, 3, 4), (24, 8, 1, 3, 4)), ((1, 3, 8, 24, 4), (3, 1, 8, 24, 4)))
CB, VB = 4, 8
F32, BF16 = jnp.float32, jnp.bfloat16
VMEM, SMEM = pl.BlockSpec(memory_space=pltpu.VMEM), pl.BlockSpec(memory_space=pltpu.SMEM)

def code_of(place, kpoint):
    index, core = place[0], place[1]
    x, z, y = index >> 3, (index >> 2) & 1, index & 3

    first, second = (x, y) if kpoint == 0 else (y, x)
    one, two = (first ^ (first >> 1)) & 1, first >> 1
    quarter = (one << 1 | two) + ((two << 1 | one) - (one << 1 | two)) * core
    return quarter, ((second ^ (second >> 1)) & 1) << 2 | (second >> 1) << 1 | z


def swap(value, axis, mask):
    return lax.ppermute(value, axis, [(i, i ^ mask) for i in range(lax.axis_size(axis))])


def cross(value, kpoint, *dims):
    groups, ways = lax.axis_size("ka"), lax.axis_size("wa")
    pairs = []
    for group in range(groups):
        mask = 0
        for dim in dims:
            mask ^= MASKS[kpoint][group & 1][dim]
        pairs += [(group * ways + i, group * ways + (i ^ mask)) for i in range(ways)]
    return lax.ppermute(value, ("ka", "wa"), pairs)


def around(value, kpoint, dim):
    return swap(value, "wa", MASKS[kpoint][0][dim])


def everyone(value, axis):
    parts = lax.axis_size(axis)
    return lax.all_to_all(jnp.broadcast_to(value[None], (parts,) + value.shape), axis, 0, 0)


def gathered_chunks(kpoint, partial, factor):
    own, second, first, both = partial
    second = second + cross(both, kpoint, 0)
    one, two = cross(first, kpoint, 0), cross(second, kpoint, 1)

    def summed(place):
        lines = slice(2 * place, 2 * place + 2)
        return (own[lines] + one[lines]) + two[lines]

    held = (summed(0) + cross(summed(2), kpoint, 2)) + (
        cross(summed(1), kpoint, 3) + cross(summed(3), kpoint, 2, 3)
    )
    held = (held + cross(held, kpoint, 4)[::-1]) * factor
    others = [cross(held, kpoint, *dims) for dims in ((3,), (2,), (2, 3))]
    held = jnp.concatenate([held] + others)
    return held, around(held, kpoint, 1), around(held, kpoint, 0)


def momentum_kernel(kpoint, quarters, place_ref, val_ref, miller_ref, cond_ref, *refs):
    outs, weighted = refs[:-1], refs[-1]
    nval = val_ref.shape[1]
    rows, cols = outs[0].shape[2:]
    me_c, me_v = code_of(place_ref, kpoint)
    for place in range(VB):
        source = pl.multiple_of((place ^ me_v) * rows, rows)
        block = val_ref[kpoint, pl.ds(source, rows), :].astype(F32)
        for axis in range(3):
            factor = miller_ref[axis : axis + 1, :].astype(F32)
            weighted[axis * nval + place * rows : axis * nval + (place + 1) * rows, :] = (
                block * factor
            ).astype(BF16)
    for quarter, out in zip(quarters, outs):
        start = pl.multiple_of((quarter ^ me_c) * cols, cols)
        result = lax.dot_general(
            weighted[...],
            cond_ref[kpoint, pl.ds(start, cols), :],
            (((1,), (1,)), ((), ())),
            preferred_element_type=F32,
        )
        for eighth in range(VB):
            for axis in range(3):
                start = axis * nval + eighth * rows
                out[eighth, axis] = result[start : start + rows]


def partial_momentum(kpoint, quarters, place, coeff_val, miller, coeff_cond):
    _, nval, depth = coeff_val.shape
    ncond = coeff_cond.shape[1]
    count = len(quarters)
    return pl.pallas_call(
        functools.partial(momentum_kernel, kpoint, quarters),
        out_shape=[jax.ShapeDtypeStruct((VB, 3, nval // VB, ncond // CB), F32)] * count,
        in_specs=[SMEM, VMEM, VMEM, VMEM],
        out_specs=[VMEM] * count,
        scratch_shapes=[pltpu.VMEM((3 * nval, depth), BF16)],
        cost_estimate=pl.CostEstimate(
            flops=2 * 3 * nval * ncond * depth * count // CB,
            bytes_accessed=(2 * nval + 2 * ncond * count // CB) * depth + 12 * nval * ncond * count // CB,
            transcendentals=0,
        ),
        compiler_params=pltpu.CompilerParams(vmem_limit_bytes=24 << 20),
        name="partial_momentum",
    )(place, coeff_val, miller, coeff_cond)


def pair_kernel(groups, place_ref, weight_ref, freq_ref, energy_val, energy_cond, orbit_val, orbit_cond, *refs):
    _, nval, points = orbit_val.shape
    ncond = orbit_cond.shape[1]
    nfreq = freq_ref.shape[0]
    count = sum(len(quarters) for _, quarters in groups)
    chunks, refs = refs[:count], refs[count:]
    begins = groups[0][1][0] == 0
    before, refs = (None, refs) if begins else (refs[0], refs[1:])
    outs, (total, amplitude, level, orbits, weight) = refs[:-5], refs[-5:]
    rows, cols = chunks[0].shape[2:]
    scale = float(nval * ncond) ** (-0.5)
    tops = 3 * nfreq
    for spot, (k, quarters) in enumerate(groups):
        mine, chunks = chunks[: len(quarters)], chunks[len(quarters) :]
        depth = len(quarters) * cols
        me_c, me_v = code_of(place_ref, k)
        level[spot] = jnp.transpose(jnp.broadcast_to(energy_val[k : k + 1, :], (nval, nval)))
        top = []
        for part, quarter in enumerate(quarters):
            if quarter in (1, 2):
                quarter = quarter + (3 - 2 * quarter) * place_ref[1]
            start = pl.multiple_of((quarter ^ me_c) * cols, cols)
            top.append(energy_cond[k : k + 1, pl.ds(start, cols)])
            orbits[spot, part * cols : (part + 1) * cols, :] = orbit_cond[k, pl.ds(start, cols), :]

        def bottom_of(where, spot=spot):
            return jnp.concatenate([level[spot, where, :]] * (cols // nval), axis=1)

        def factors_of(gap):
            square = gap * gap
            return [4.0 / (square + freq_ref[w] * freq_ref[w]) for w in range(nfreq)]

        def eighth(place, carry, k=k, spot=spot, me_v=me_v, top=top, mine=mine, bottom_of=bottom_of):
            here = pl.ds(pl.multiple_of(place * rows, rows), rows)
            there = pl.ds(pl.multiple_of((place ^ me_v) * rows, rows), rows)
            weight[spot, here, :] = orbit_val[k, there, :].astype(F32) * (weight_ref[k] * scale)
            bottom = bottom_of(there)
            for part, chunk in enumerate(mine):
                factors = factors_of(top[part] - bottom)
                for axis in range(3):
                    momentum = chunk[place, axis]
                    for w in range(nfreq):
                        start = pl.multiple_of((axis * nfreq + w) * nval + place * rows, rows)
                        amplitude[spot, pl.ds(start, rows), part * cols : (part + 1) * cols] = (
                            momentum * factors[w]
                        ).astype(BF16)
            return carry

        lax.fori_loop(0, VB, eighth, 0, unroll=2)
        for axis in range(3):
            start = axis * nfreq * nval
            expanded = jnp.dot(
                amplitude[spot, start : start + nfreq * nval, :depth],
                orbits[spot, :depth, :],
                preferred_element_type=F32,
            )
            for w in range(nfreq):
                row = slice(axis * nfreq + w, axis * nfreq + w + 1)
                value = jnp.sum(expanded[w * nval : (w + 1) * nval] * weight[spot], axis=0, keepdims=True)
                if spot > 0:
                    value = value + total[row, :]
                elif not begins:
                    value = value + before[row, :]
                total[row, :] = value

        if begins:
            bottom = bottom_of(pl.ds(pl.multiple_of(me_v * rows, rows), rows))
            gap = top[0] - bottom
            ratios = [factor / gap for factor in factors_of(gap)]
            for axis in range(3):
                square = mine[0][0, axis] * mine[0][0, axis]
                row = slice(tops + axis, tops + axis + 1)
                for w in range(nfreq):
                    value = jnp.sum(square * ratios[w], axis=0, keepdims=True)
                    value = (value[:, :nval] + value[:, nval:]) * (weight_ref[k] / float(nval * ncond))
                    lanes = slice(w * nval, (w + 1) * nval)
                    total[row, lanes] = value + total[row, lanes] if spot else value
            row = slice(tops + 3, tops + 4)
            value = jnp.full((1, points), weight_ref[k], F32)
            total[row, :] = value + total[row, :] if spot else value
    if not begins:
        total[tops:, :] = before[tops:, :]
    if len(outs) == 2:
        keep, send = outs
        across = points // 2
        keep[...] = total[:, pl.ds(pl.multiple_of(place_ref[1] * across, across), across)]
        send[...] = total[:, pl.ds(pl.multiple_of((1 - place_ref[1]) * across, across), across)]
    else:
        outs[0][...] = total[...]


def pair_sums(groups, place, weights, freqs, energy_val, energy_cond, orbit_val, orbit_cond, chunks, before, parts):
    _, nval, points = orbit_val.shape
    ncond = orbit_cond.shape[1]
    nfreq = freqs.shape[0]
    height = 3 * nfreq + 4
    depth = ncond // CB * max(len(quarters) for _, quarters in groups)
    count = len(groups)
    operands = [energy_val, energy_cond, orbit_val, orbit_cond]
    operands += [chunks[k][quarter] for k, quarters in groups for quarter in quarters]
    operands += before
    return list(
        pl.pallas_call(
            functools.partial(pair_kernel, groups),
            out_shape=[jax.ShapeDtypeStruct((height, points // parts), F32)] * parts,
            in_specs=[SMEM] * 3 + [VMEM] * len(operands),
            out_specs=[VMEM] * parts,
            scratch_shapes=[
                pltpu.VMEM((height, points), F32),
                pltpu.VMEM((count, 3 * nfreq * nval, depth), BF16),
                pltpu.VMEM((count, nval, nval), F32),
                pltpu.VMEM((count, depth, points), BF16),
                pltpu.VMEM((count, nval, points), F32),
            ],
            cost_estimate=pl.CostEstimate(
                flops=count * 2 * 3 * nfreq * nval * depth * points,
                bytes_accessed=count * (12 * nval * depth + 4 * depth * points),
                transcendentals=0,
            ),
            compiler_params=pltpu.CompilerParams(vmem_limit_bytes=20 << 20),
            name="pair_sums",
        )(place, weights, freqs, *operands)
    )


def wing_kernel(place_ref, gathered, zeta, out):
    ways, height, points = gathered.shape
    slab_rows = zeta.shape[0]
    tops = height - 4
    total = jnp.zeros((3 * height, slab_rows), F32)
    last = jnp.zeros((4, points), F32)
    for device in range(ways):
        value = gathered[device]
        last = last + value[tops:]
        pieces = []
        for _ in range(3):
            rounded = value.astype(BF16)
            pieces.append(rounded)
            value = value - rounded.astype(F32)
        start = pl.multiple_of((2 * device + place_ref[1]) * points, points)
        total = total + lax.dot_general(
            jnp.concatenate(pieces, axis=0),
            zeta[:, pl.ds(start, points)],
            (((1,), (1,)), ((), ())),
            preferred_element_type=F32,
        )
    total = total[:height] + total[height : 2 * height] + total[2 * height :]
    out[:tops] = total[:tops]
    lane = lax.broadcasted_iota(jnp.int32, (3, slab_rows), 1)
    across = points // 2
    head = jnp.zeros((3, slab_rows), F32)
    for tile in range(2):
        value = jnp.sum(last[:3, tile * across : (tile + 1) * across], axis=1, keepdims=True)
        head = jnp.where(lane == 2 * place_ref[1] + tile, value, head)
    out[tops : tops + 3] = head
    out[tops + 3 :] = last[3:, :slab_rows]


def wing_sums(place, gathered, zeta):
    ways, height, points = gathered.shape
    slab_rows = zeta.shape[0]
    return pl.pallas_call(
        wing_kernel,
        out_shape=jax.ShapeDtypeStruct((height, slab_rows), F32),
        in_specs=[SMEM, VMEM, VMEM],
        out_specs=VMEM,
        cost_estimate=pl.CostEstimate(
            flops=6 * height * slab_rows * ways * points,
            bytes_accessed=4 * slab_rows * ways * points + 4 * height * ways * points,
            transcendentals=0,
        ),
        compiler_params=pltpu.CompilerParams(vmem_limit_bytes=20 << 20),
        name="wing_sums",
    )(place, gathered, zeta)


def final_kernel(copies, one, two, wing, head):
    total = one[...] + two[...]
    tops = total.shape[0] - 4
    nfreq = wing.shape[1]
    scale = copies / total[tops + 3 :]
    for axis in range(3):
        wing[axis] = total[axis * nfreq : (axis + 1) * nfreq] * scale
    head[...] = total[tops : tops + 3, :nfreq] * scale[:, :nfreq]


def local(
    coeff_val,
    coeff_cond,
    miller,
    energy_val,
    energy_cond,
    orbit_val,
    orbit_cond,
    zeta,
    freqs,
    kweight,
):
    kcount, nval, npw_dev = coeff_val.shape
    nfreq = freqs.shape[0]
    slab_rows = zeta.shape[0]
    ways = lax.axis_size("wa")
    pw_factor = float(npw_dev * ways) ** (-0.5)
    weights = kweight.astype(F32)
    place = jnp.stack([lax.axis_index("wa"), lax.axis_index("ka") & 1]).astype(jnp.int32)

    operands = (place, coeff_val, miller, coeff_cond)
    sends = [partial_momentum(k, (3, 2), *operands) for k in range(kcount)]
    keeps = [partial_momentum(k, (1, 0), *operands) for k in range(kcount)]
    parts = [(own, second, first, both) for (both, first), (second, own) in zip(sends, keeps)]
    chunks = [gathered_chunks(k, parts[k], pw_factor) for k in range(kcount)]
    operands = (place, weights, freqs, energy_val, energy_cond, orbit_val, orbit_cond)
    pair = pair_sums(((0, (0,)), (1, (0,))), *operands, chunks, [], 1)
    for k in range(kcount):
        own, second, first = chunks[k]
        if k == 0:
            first, pair = lax.optimization_barrier((first, pair))
        half = first.shape[0] // 2
        passed = jnp.concatenate([around(first[:half], k, 1), around(second[half:], k, 0)])
        chunks[k] = (own, second, first, passed)
    for k in range(kcount):
        pair = pair_sums(((k, (1, 2)),), *operands, chunks, pair, 1)
    keep, send = pair_sums(((0, (3,)), (1, (3,))), *operands, chunks, pair, 2)
    pair = keep + swap(send, "ka", 1)
    total = wing_sums(place, everyone(pair, "wa"), zeta)
    total = total + swap(total, "ka", 1)
    total = total + swap(total, "ka", 2)
    return pl.pallas_call(
        functools.partial(final_kernel, float(2 * ways)),
        out_shape=[
            jax.ShapeDtypeStruct((3, nfreq, slab_rows), F32),
            jax.ShapeDtypeStruct((3, nfreq), F32),
        ],
        in_specs=[VMEM] * 2,
        out_specs=[VMEM] * 2,
        compiler_params=pltpu.CompilerParams(vmem_limit_bytes=4 << 20),
        name="final",
    )(total, swap(total, "ka", 6))


def solution(mesh):
    return jax.shard_map(
        local,
        mesh=mesh,
        in_specs=(
            P("ka", None, "wa"),
            P("ka", None, "wa"),
            P(None, "wa"),
            P("ka", None),
            P("ka", None),
            P("ka", None, "wa"),
            P("ka", None, "wa"),
            P("wa", None),
            P(),
            P("ka"),
        ),
        out_specs=(P(None, None, "wa"), P()),
        check_vma=False,
    )
```
